256 devices in a mesh: client: 8 (over z), row: 8 (over y, core), col: 4 (over x).
Axes of the slice: x: 4, y: 4, z: 8, core: 2. Of those that a mesh axis runs over, the one named last changes fastest.
Arguments:
- client_acts: bfloat16 [8, 512, 7168], P('client', 'col', 'row'), may hold values from -10 to 10
- anchor_acts: bfloat16 [512, 7168], P('row', 'col'), may hold values from -10 to 10
- client_weights: bfloat16 [8, 2048, 7168], P('client', 'col', 'row'), may hold values from -12 to 12
Outputs:
- joined: bfloat16 [2048, 7168], P(('client', 'row'), 'col')
The draws below stay inside these ranges and needn't reach their ends.
All inputs are finite; a program needn't handle non-finite values.
Results may differ from the reference program's by a relative error of at most 0.0049.
Values may be sent and summed in bfloat16 or wider, within the bound.
No kernel may reach another device: no remote copies, remote signals or barrier semaphores. Data moves between devices by JAX's collectives and lax.ppermute only.
A program may use at most 128 MiB of HBM per device.

```python
import math
import jax
import jax.numpy as jnp
from jax import lax

D = 2048
FF = 7168
TOK = 512
ITERS = 3
CLIENTS = 8


def scaled_columns(key, shape, spread_lo, spread_hi):
    key_scale, key_value = jax.random.split(key)
    scale_shape = shape[:-2] + (1, shape[-1])
    scales = jnp.exp(jax.random.uniform(key_scale, scale_shape, jnp.float32, math.log(spread_lo), math.log(spread_hi)))
    values = jax.random.truncated_normal(key_value, -4.0, 4.0, shape, jnp.float32)
    return (values * scales).astype(jnp.bfloat16)


def draw_client_acts(key, part):
    key = jax.random.fold_in(key, 11)
    return scaled_columns(key, (CLIENTS, TOK, FF), 0.5, 2.5)


def draw_anchor_acts(key, part):
    key = jax.random.fold_in(key, 23)
    return scaled_columns(key, (TOK, FF), 0.5, 2.5)


def with_spikes(array, key, source, target, parts, factor):
    owner, partner = [(jnp.arange(array.shape[dim]) // (array.shape[dim] // parts)).reshape([-1 if axis == dim else 1 for axis in range(array.ndim)]) for dim in (source, target)]
    chosen = jax.random.permutation(key, parts)[partner]
    strong = (owner == chosen) | (owner == (partner + parts // 2) % parts)
    return jnp.where(strong, factor * array, array)


def level_of(rng, extent, cuts, smallest, largest):
    def one(position, shards_of):
        steps = jax.random.uniform(jax.random.fold_in(jax.random.fold_in(rng, 6), position), (shards_of,), jnp.float32, smallest / len(cuts), largest / len(cuts))
        return jnp.repeat(jnp.exp(steps), extent[position] // shards_of).reshape((-1,) + (1,) * (len(extent) - position - 1))

    loudness = one(*cuts[0])
    for cut in cuts[1:]:
        loudness = loudness * one(*cut)
    return loudness


def heavy_noise(own_key, extent, spread, most, shards, heavy, dtype=jnp.bfloat16):
    result = spread * jax.random.normal(own_key, extent, jnp.float32)
    if shards:
        result = result * level_of(own_key, extent, shards, -0.22, 0.18)
    return jnp.clip(with_spikes(result, jax.random.fold_in(own_key, 3), *heavy), -most, most).astype(dtype)


def setup_inputs(seed: int = 0) -> dict:
    splits = jax.random.split(jax.random.key(seed), 4)
    return {
        "client_acts": draw_client_acts(jax.random.fold_in(splits[3], 71), 0),
        "anchor_acts": draw_anchor_acts(jax.random.fold_in(splits[3], 71), 0),
        "client_weights": heavy_noise(splits[2], (CLIENTS, D, FF), 2.0, 12.0, ((0, 8), (1, 4), (2, 8)), (2, 1, 8, 2.0)),
    }


entropic = 0.05


def align_one(acts, anchor_acts, weights):
    similarity = jnp.dot(acts.T, anchor_acts, preferred_element_type=jnp.float32)
    kernel = jnp.exp(similarity / (TOK * entropic))
    col_scale = jnp.ones((FF,), jnp.float32)
    row_scale = jnp.ones((FF,), jnp.float32)
    for step in range(ITERS):
        row_scale = (1.0 / FF) / jnp.dot(kernel, col_scale, precision=lax.Precision.HIGHEST)
        col_scale = (1.0 / FF) / jnp.dot(row_scale, kernel, precision=lax.Precision.HIGHEST)
    plan = (FF * row_scale[:, None] * kernel * col_scale[None, :]).astype(jnp.bfloat16)
    return jnp.dot(weights, plan, preferred_element_type=jnp.float32)


def reference(client_acts, anchor_acts, client_weights):
    total = jnp.zeros((D, FF), jnp.float32)
    for index in range(CLIENTS):
        total = total + align_one(client_acts[index], anchor_acts, client_weights[index])
    return (total / CLIENTS).astype(jnp.bfloat16)
```

```python
import jax
import jax.numpy as jnp
from jax import lax
from jax.experimental import pallas as pl
from jax.experimental.pallas import tpu as pltpu
from jax.sharding import Mesh, PartitionSpec as P

FF = 7168
TOK = 512
ITERS = 3
CLIENTS = 8
entropic = 0.05

F32 = jnp.float32
BF16 = jnp.bfloat16
SIZES = {"client": 8, "y": 4, "core": 2, "col": 4}
ROWS = 896
COLS = 1792
RB = ROWS // 128
CT = 256


def shift(x, axis, s):
    n = SIZES[axis]
    return lax.ppermute(x, axis, [(i, (i + s) % n) for i in range(n)])


def params(mb):
    return pltpu.CompilerParams(vmem_limit_bytes=mb * 1024 * 1024)


def rows_to_lanes(acc_ref, out_ref):
    for b in range(RB):
        block = acc_ref[pl.ds(b * 128, 128), :]
        out_ref[pl.ds(b, 1), :] = jnp.sum(block.T, axis=0, keepdims=True)
    out_ref[pl.ds(RB, 1), :] = jnp.ones((1, 128), F32)


def first_kernel(place_ref, *refs):
    a = refs[0:4]
    b = refs[4:8]
    o = refs[8:12]
    k_ref, rp_ref, acts_ref, anchor_ref, acc_ref = refs[12:]
    off = place_ref[0]
    core = place_ref[1]
    for s in range(4):
        acts_ref[pl.ds(128 * s, 128), :] = a[s][...]
        at = lax.rem(s + off, 4) * 128
        anchor_ref[pl.ds(pl.multiple_of(at + 64 * core, 64), 64), :] = b[s][...]
        anchor_ref[pl.ds(pl.multiple_of(at + 64 * (1 - core), 64), 64), :] = o[s][...]
    for t in range(COLS // CT):
        sim = lax.dot_general(
            acts_ref[...], anchor_ref[:, t * CT:(t + 1) * CT],
            (((0,), (0,)), ((), ())), preferred_element_type=F32)
        k = jnp.exp(sim * (1.0 / (TOK * entropic)))
        k_ref[:, t * CT:(t + 1) * CT] = k
        part = k[:, :128] + k[:, 128:]
        if t == 0:
            acc_ref[...] = part
        else:
            acc_ref[...] += part
    rows_to_lanes(acc_ref, rp_ref)


def first(place, a, b, o):
    vm = pl.BlockSpec(memory_space=pltpu.VMEM)
    return pl.pallas_call(
        first_kernel,
        in_specs=[pl.BlockSpec(memory_space=pltpu.SMEM)] + [vm] * 12,
        out_specs=[vm] * 4,
        out_shape=[
            jax.ShapeDtypeStruct((ROWS, COLS), F32),
            jax.ShapeDtypeStruct((8, 128), F32),
            jax.ShapeDtypeStruct((TOK, ROWS), BF16),
            jax.ShapeDtypeStruct((TOK, COLS), BF16),
        ],
        scratch_shapes=[pltpu.VMEM((ROWS, 128), F32)],
        compiler_params=params(24),
        cost_estimate=pl.CostEstimate(flops=2 * TOK * ROWS * COLS, bytes_accessed=10_000_000, transcendentals=ROWS * COLS),
        name="similarity",
    )(place, *a, *b, *o)


def spread(r, b):
    return jnp.broadcast_to(r[b:b + 1, :], (128, 128)).T


def col_kernel(k_ref, p0, p1, p2, p3, r_ref, cp_ref):
    r = (1.0 / FF) / (p0[...] + p1[...] + p2[...] + p3[...])
    r_ref[...] = r
    acc = jnp.zeros((8, COLS), F32)
    for b in range(RB):
        rb = spread(r, b)
        for g in range(16):
            scale = rb[8 * g:8 * g + 8, :]
            row = k_ref[pl.ds(b * 128 + g * 8, 8), :]
            acc = acc + row * jnp.concatenate([scale] * (COLS // 128), axis=1)
    cp_ref[...] = jnp.sum(acc, axis=0, keepdims=True)


def col_pass(k, parts):
    vm = pl.BlockSpec(memory_space=pltpu.VMEM)
    return pl.pallas_call(
        col_kernel,
        in_specs=[vm] * 5,
        out_specs=[vm] * 2,
        out_shape=[jax.ShapeDtypeStruct((8, 128), F32), jax.ShapeDtypeStruct((1, COLS), F32)],
        compiler_params=params(12),
        cost_estimate=pl.CostEstimate(flops=2 * ROWS * COLS, bytes_accessed=6_500_000, transcendentals=0),
        name="column_sums",
    )(k, *parts)


def row_kernel(k_ref, p0, p1, p2, p3, c_ref, rp_ref, acc_ref):
    c = (1.0 / FF) / (p0[...] + p1[...] + p2[...] + p3[...])
    c_ref[...] = c
    for g in range(ROWS // 32):
        acc = jnp.zeros((32, 128), F32)
        for t in range(COLS // 128):
            acc = acc + k_ref[pl.ds(32 * g, 32), t * 128:(t + 1) * 128] * c[:, t * 128:(t + 1) * 128]
        acc_ref[pl.ds(32 * g, 32), :] = acc
    rows_to_lanes(acc_ref, rp_ref)


def row_pass(k, parts):
    vm = pl.BlockSpec(memory_space=pltpu.VMEM)
    return pl.pallas_call(
        row_kernel,
        in_specs=[vm] * 5,
        out_specs=[vm] * 2,
        out_shape=[jax.ShapeDtypeStruct((1, COLS), F32), jax.ShapeDtypeStruct((8, 128), F32)],
        scratch_shapes=[pltpu.VMEM((ROWS, 128), F32)],
        compiler_params=params(12),
        cost_estimate=pl.CostEstimate(flops=2 * ROWS * COLS, bytes_accessed=6_500_000, transcendentals=0),
        name="row_sums",
    )(k, *parts)


def more_kernel(acts_ref, anchor_ref, k_ref):
    for t in range(COLS // CT):
        sim = lax.dot_general(
            acts_ref[...], anchor_ref[:, t * CT:(t + 1) * CT],
            (((0,), (0,)), ((), ())), preferred_element_type=F32)
        k_ref[:, t * CT:(t + 1) * CT] = jnp.exp(sim * (1.0 / (TOK * entropic))).astype(BF16)


def more(acts, anchor):
    vm = pl.BlockSpec(memory_space=pltpu.VMEM)
    return pl.pallas_call(
        more_kernel,
        in_specs=[vm] * 2,
        out_specs=vm,
        out_shape=jax.ShapeDtypeStruct((ROWS, COLS), BF16),
        compiler_params=params(16),
        cost_estimate=pl.CostEstimate(flops=2 * TOK * ROWS * COLS, bytes_accessed=6_000_000, transcendentals=ROWS * COLS),
        name="more_rows",
    )(acts, anchor)


def join_kernel(w_ref, k0, k1, k2, k3, r0, r1, r2, r3, c_ref, out_ref, lhs_ref, rb_ref, p_ref):
    ks = (k0, k1, k2, k3)

    @pl.when(pl.program_id(0) == 0)
    def _():
        for s, r in enumerate((r0, r1, r2, r3)):
            rr = r[...] * FF
            for b in range(RB):
                rb_ref[pl.ds(s * ROWS + b * 128, 128), :] = spread(rr, b)
            for t in range(4):
                for e in range(2):
                    for h in range(2):
                        lhs_ref[pl.ds(h * 256 + (2 * t + e) * 32, 32), s * ROWS:(s + 1) * ROWS] = (
                            w_ref[t, s, e, pl.ds(32 * h, 32), :])

    c = c_ref[...]
    for s in range(4):
        rb = rb_ref[pl.ds(s * ROWS, ROWS), :]
        for h in range(CT // 128):
            lanes = slice(h * 128, (h + 1) * 128)
            p_ref[pl.ds(s * ROWS, ROWS), lanes] = (rb * ks[s][:, lanes].astype(F32) * c[:, lanes]).astype(BF16)
    out_ref[...] = jnp.dot(lhs_ref[...], p_ref[...], preferred_element_type=F32)


def join(w, ks, rs, c):
    vm = pl.BlockSpec(memory_space=pltpu.VMEM)
    return pl.pallas_call(
        join_kernel,
        grid=(COLS // CT,),
        in_specs=[vm] + [pl.BlockSpec((ROWS, CT), lambda i: (0, i))] * 4 + [vm] * 4 + [pl.BlockSpec((1, CT), lambda i: (0, i))],
        out_specs=pl.BlockSpec((512, CT), lambda i: (0, i)),
        out_shape=jax.ShapeDtypeStruct((512, COLS), F32),
        scratch_shapes=[pltpu.VMEM((512, 4 * ROWS), BF16), pltpu.VMEM((4 * ROWS, 128), F32), pltpu.VMEM((4 * ROWS, CT), BF16)],
        compiler_params=params(36),
        cost_estimate=pl.CostEstimate(flops=2 * 512 * 4 * ROWS * COLS, bytes_accessed=20_000_000, transcendentals=0),
        name="join",
    )(w, *ks, *rs, c)


def pick(x, index, axis):
    return lax.dynamic_index_in_dim(x, index, axis, keepdims=False)


def local(client_acts, anchor_acts, client_weights):
    z = lax.axis_index("client")
    y = lax.axis_index("y")
    core = lax.axis_index("core")
    x = lax.axis_index("col")
    acts = client_acts[0]

    a = [acts] + [shift(acts, "col", s) for s in (1, 2, 3)]
    b = [anchor_acts] + [shift(anchor_acts, "y", s) for s in (1, 2, 3)]
    o = [shift(v, "core", 1) for v in b]

    w = client_weights[0].reshape(2, 4, 64, ROWS)
    w = [pick(w, lax.rem(y + s, 4), 1) for s in range(4)]
    w = jnp.stack([w[0]] + [shift(w[s], "y", s) for s in (1, 2, 3)])
    w = lax.all_gather(w, "col", axis=0)

    place = jnp.stack([lax.rem(x - y + 4, 4), core]).astype(jnp.int32)
    k, rp, acts_all, anchor_all = first(place, a, b, o)

    ks = [k] + [more(shift(acts_all, "y", s), anchor_all) for s in (1, 2, 3)]

    c = None
    for step in range(ITERS):
        r, cp = col_pass(k, [rp] + [shift(rp, "col", s) for s in (1, 2, 3)])
        cp = cp + shift(cp, "core", 1)
        cps = [cp] + [shift(cp, "y", s) for s in (1, 2, 3)]
        if step < ITERS - 1:
            c, rp = row_pass(k, cps)
    rs = [r] + [shift(r, "y", s) for s in (1, 2, 3)]
    ratio = (1.0 / FF) / (cps[0] + cps[1] + cps[2] + cps[3]) / c

    total = join(w, ks, rs, c).reshape(2, 8, 32, COLS)
    sib = (pick(total, 1 - core, 0) * ratio).astype(BF16)
    mine = pick(total, core, 0) * ratio + shift(sib, "core", 1).astype(F32)
    out = pick(mine, z, 0)
    mine = mine.astype(BF16)
    for s in (4, 3, 5, 2, 6, 1, 7):
        out = out + shift(pick(mine, lax.rem(z + s, 8), 0), "client", s).astype(F32)
    return (out / CLIENTS).astype(BF16)


def solution(mesh):
    mesh = Mesh(mesh.devices.reshape(8, 4, 2, 4), ("client", "y", "core", "col"))
    row = ("y", "core")
    in_specs = (P("client", "col", row), P(row, "col"), P("client", "col", row))
    out_specs = P(("client", "y", "core"), "col")
    return jax.shard_map(local, mesh=mesh, in_specs=in_specs, out_specs=out_specs, check_vma=False)
```

```python
import functools

import jax
import jax.numpy as jnp
from jax import lax
from jax.experimental import pallas as pl
from jax.experimental.pallas import tpu as pltpu
from jax.sharding import Mesh, PartitionSpec as P

FF = 7168
TOK = 512
ITERS = 3
CLIENTS = 8
entropic = 0.05

F32 = jnp.float32
BF16 = jnp.bfloat16
SIZES = {"client": 8, "y": 4, "core": 2, "col": 4}
ROWS = 896
COLS = 1792
RB = ROWS // 128
CT = 256


def shift(x, axis, s):
    n = SIZES[axis]
    return lax.ppermute(x, axis, [(i, (i + s) % n) for i in range(n)])


def params(mb):
    return pltpu.CompilerParams(vmem_limit_bytes=mb * 1024 * 1024)


def rows_to_lanes(acc_ref, out_ref):
    for b in range(RB):
        block = acc_ref[pl.ds(b * 128, 128), :]
        out_ref[pl.ds(b, 1), :] = jnp.sum(block.T, axis=0, keepdims=True)
    out_ref[pl.ds(RB, 1), :] = jnp.ones((1, 128), F32)


def first_kernel(place_ref, *refs):
    a = refs[0:4]
    b = refs[4:8]
    o = refs[8:12]
    k_ref, rp_ref, lo_ref, hi_ref, anchor_ref, acc_ref, acts_ref = refs[12:]
    off = place_ref[0]
    core = place_ref[1]
    for s in range(4):
        acts_ref[pl.ds(128 * s, 128), :] = a[s][...]
        (lo_ref, hi_ref)[s // 2][pl.ds(128 * (s % 2), 128), :] = a[s][...]
        at = lax.rem(s + off, 4) * 128
        anchor_ref[pl.ds(pl.multiple_of(at + 64 * core, 64), 64), :] = b[s][...]
        anchor_ref[pl.ds(pl.multiple_of(at + 64 * (1 - core), 64), 64), :] = o[s][...]
    for t in range(COLS // CT):
        sim = lax.dot_general(
            acts_ref[...], anchor_ref[:, t * CT:(t + 1) * CT],
            (((0,), (0,)), ((), ())), preferred_element_type=F32)
        k = jnp.exp(sim * (1.0 / (TOK * entropic)))
        k_ref[:, t * CT:(t + 1) * CT] = k
        part = k[:, :128] + k[:, 128:]
        if t == 0:
            acc_ref[...] = part
        else:
            acc_ref[...] += part
    rows_to_lanes(acc_ref, rp_ref)


VM = pl.BlockSpec(memory_space=pltpu.VMEM)
ANY = pl.BlockSpec(memory_space=pl.ANY)


def first(place, a, b, o):
    return pl.pallas_call(
        first_kernel,
        in_specs=[pl.BlockSpec(memory_space=pltpu.SMEM)] + [VM] * 12,
        out_specs=[VM] * 5,
        out_shape=[
            jax.ShapeDtypeStruct((ROWS, COLS), F32),
            jax.ShapeDtypeStruct((8, 128), F32),
            jax.ShapeDtypeStruct((TOK // 2, ROWS), BF16),
            jax.ShapeDtypeStruct((TOK // 2, ROWS), BF16),
            jax.ShapeDtypeStruct((TOK, COLS), BF16),
        ],
        scratch_shapes=[pltpu.VMEM((ROWS, 128), F32), pltpu.VMEM((TOK, ROWS), BF16)],
        compiler_params=params(24),
        cost_estimate=pl.CostEstimate(flops=2 * TOK * ROWS * COLS, bytes_accessed=10_000_000, transcendentals=ROWS * COLS),
        name="similarity",
    )(place, *a, *b, *o)


def spread(r, b):
    return jnp.broadcast_to(r[b:b + 1, :], (128, 128)).T


def col_kernel(n, k_ref, p_ref, *refs):
    r_ref, cp_ref = refs[n:n + 2]
    r = (1.0 / FF) / p_ref[...]
    r_ref[...] = r
    acc = jnp.zeros((8, COLS), F32)
    for b in range(RB):
        rb = spread(r, b)
        for g in range(16):
            scale = rb[8 * g:8 * g + 8, :]
            row = k_ref[pl.ds(b * 128 + g * 8, 8), :]
            acc = acc + row * jnp.concatenate([scale] * (COLS // 128), axis=1)
    cp_ref[...] = jnp.sum(acc, axis=0, keepdims=True)


def like(v):
    return jax.ShapeDtypeStruct(v.shape, v.dtype)


def col_pass(k, part, *held):
    n = len(held)
    r, cp, *held = pl.pallas_call(
        functools.partial(col_kernel, n),
        in_specs=[VM] * 2 + [ANY] * n,
        out_specs=[VM] * 2 + [ANY] * n,
        out_shape=[jax.ShapeDtypeStruct((8, 128), F32), jax.ShapeDtypeStruct((1, COLS), F32)] + [like(v) for v in held],
        input_output_aliases={2 + i: 2 + i for i in range(n)},
        compiler_params=params(12),
        cost_estimate=pl.CostEstimate(flops=2 * ROWS * COLS, bytes_accessed=6_500_000, transcendentals=0),
        name="column_sums",
    )(k, part, *held)
    return r, cp, held


def row_kernel(n, k_ref, p_ref, *refs):
    rp_ref = refs[n]
    acc_ref = refs[-1]
    c = (1.0 / FF) / p_ref[...]
    for g in range(ROWS // 32):
        acc = jnp.zeros((32, 128), F32)
        for t in range(COLS // 128):
            acc = acc + k_ref[pl.ds(32 * g, 32), t * 128:(t + 1) * 128] * c[:, t * 128:(t + 1) * 128]
        acc_ref[pl.ds(32 * g, 32), :] = acc
    rows_to_lanes(acc_ref, rp_ref)


def row_pass(k, part, *held):
    n = len(held)
    rp, *held = pl.pallas_call(
        functools.partial(row_kernel, n),
        in_specs=[VM] * 2 + [ANY] * n,
        out_specs=[VM] + [ANY] * n,
        out_shape=[jax.ShapeDtypeStruct((8, 128), F32)] + [like(v) for v in held],
        input_output_aliases={2 + i: 1 + i for i in range(n)},
        scratch_shapes=[pltpu.VMEM((ROWS, 128), F32)],
        compiler_params=params(12),
        cost_estimate=pl.CostEstimate(flops=2 * ROWS * COLS, bytes_accessed=6_500_000, transcendentals=0),
        name="row_sums",
    )(k, part, *held)
    return rp, held


def more_kernel(a0_ref, a1_ref, anchor_ref, k_ref, lhs_ref):
    @pl.when(pl.program_id(0) == 0)
    def _():
        lhs_ref[pl.ds(0, 256), :] = a0_ref[...]
        lhs_ref[pl.ds(256, 256), :] = a1_ref[...]

    sim = lax.dot_general(lhs_ref[...], anchor_ref[...], (((0,), (0,)), ((), ())), preferred_element_type=F32)
    k_ref[...] = jnp.exp(sim * (1.0 / (TOK * entropic))).astype(BF16)


def more(acts, anchor):
    return pl.pallas_call(
        more_kernel,
        grid=(COLS // CT,),
        in_specs=[pl.BlockSpec((256, ROWS), lambda i: (0, 0))] * 2 + [pl.BlockSpec((TOK, CT), lambda i: (0, i))],
        out_specs=pl.BlockSpec((ROWS, CT), lambda i: (0, i)),
        out_shape=jax.ShapeDtypeStruct((ROWS, COLS), BF16),
        scratch_shapes=[pltpu.VMEM((TOK, ROWS), BF16)],
        compiler_params=params(40),
        cost_estimate=pl.CostEstimate(flops=2 * TOK * ROWS * COLS, bytes_accessed=6_000_000, transcendentals=ROWS * COLS),
        name="more_rows",
    )(*acts, anchor)


def join_kernel(core_ref, w00, w01, w10, w11, w20, w21, w30, w31, k0, k1, k2, k3, r0, r1, r2, r3, c_ref,
                sib_ref, own_ref, lhs_ref, rb_ref):
    ks = (k0, k1, k2, k3)
    ws = ((w00, w01), (w10, w11), (w20, w21), (w30, w31))
    core = core_ref[0]
    x = core_ref[1]

    @pl.when(pl.program_id(0) == 0)
    def _():
        for s, r in enumerate((r0, r1, r2, r3)):
            rr = r[...] * FF
            for b in range(RB):
                rb_ref[pl.ds(s * ROWS + b * 128, 128), :] = spread(rr, b)
        for t in range(4):
            at = lax.rem(x + 4 - t, 4) * 64
            for s in range(4):
                for e in range(2):
                    for h in range(2):
                        half = 1 - core if h == 0 else core
                        lhs_ref[pl.ds(pl.multiple_of(h * 256 + at + e * 32, 32), 32), s * ROWS:(s + 1) * ROWS] = (
                            ws[t][s // 2][s % 2, e, pl.ds(pl.multiple_of(32 * half, 32), 32), :])

    c = ((1.0 / FF) / c_ref[...])
    total = None
    for s in range(4):
        rb = rb_ref[pl.ds(s * ROWS, ROWS), :]
        p = jnp.concatenate(
            [(rb * ks[s][:, h * 128:(h + 1) * 128].astype(F32) * c[:, h * 128:(h + 1) * 128]).astype(BF16)
             for h in range(CT // 128)], axis=1)
        d = jnp.dot(lhs_ref[:, s * ROWS:(s + 1) * ROWS], p, preferred_element_type=F32)
        total = d if total is None else total + d
    sib_ref[...] = total[:256].astype(BF16)
    own_ref[...] = total[256:]


def join(place, w, ks, rs, c):
    tile = pl.BlockSpec((256, CT), lambda i: (0, i))
    return pl.pallas_call(
        join_kernel,
        grid=(COLS // CT,),
        in_specs=([pl.BlockSpec(memory_space=pltpu.SMEM)] + [VM] * 8
                  + [pl.BlockSpec((ROWS, CT), lambda i: (0, i))] * 4 + [VM] * 4 + [pl.BlockSpec((1, CT), lambda i: (0, i))]),
        out_specs=[tile, tile],
        out_shape=[jax.ShapeDtypeStruct((256, COLS), BF16), jax.ShapeDtypeStruct((256, COLS), F32)],
        scratch_shapes=[pltpu.VMEM((512, 4 * ROWS), BF16), pltpu.VMEM((4 * ROWS, 128), F32)],
        compiler_params=params(48),
        cost_estimate=pl.CostEstimate(flops=2 * 512 * 4 * ROWS * COLS, bytes_accessed=20_000_000, transcendentals=0),
        name="join",
    )(place, *w, *ks, *rs, c)


def pick(x, index, axis):
    return lax.dynamic_index_in_dim(x, index, axis, keepdims=False)


def sum_over_clients(part, z):
    def at(s):
        return pick(part, lax.rem(z + 8 + s, 8), 0)

    def wide(v):
        return v.astype(F32)

    far = at(4)
    f1 = shift(far[:16], "client", -2)
    f2 = shift(far[16:], "client", 2)
    u3 = shift(at(-3), "client", -1)
    d3 = shift(at(3), "client", 1)
    u = wide(at(-2)) + wide(u3)
    u = jnp.concatenate([u[:16] + wide(f1), u[16:]], 0).astype(BF16)
    d = wide(at(2)) + wide(d3)
    d = jnp.concatenate([d[:16], d[16:] + wide(f2)], 0).astype(BF16)
    u2 = shift(u, "client", -2)
    d2 = shift(d, "client", 2)
    u1 = shift(at(-1), "client", -1)
    d1 = shift(at(1), "client", 1)
    return wide(at(0)) + wide(u1) + wide(d1) + wide(u2) + wide(d2)


def local(client_acts, anchor_acts, client_weights):
    z = lax.axis_index("client")
    y = lax.axis_index("y")
    core = lax.axis_index("core")
    x = lax.axis_index("col")
    acts = client_acts[0]

    b = [anchor_acts] + [shift(anchor_acts, "y", s) for s in (1, 2, 3)]
    a = [acts] + [shift(acts, "col", s) for s in (1, 2, 3)]
    o = [shift(v, "core", 1) for v in b]

    later = (b[1][0, 0].astype(F32) * 0.0).astype(jnp.int32)
    w = client_weights[0].reshape(2, 4, 64, ROWS)
    w = [pick(w, lax.rem(y + s, 4) + later, 1) for s in range(4)]
    w = [w[0]] + [shift(w[s], "y", s) for s in (1, 2, 3)]

    place = jnp.stack([lax.rem(x - y + 4, 4), core]).astype(jnp.int32)
    k, rp, lo, hi, anchor = first(place, a, b, o)

    def both(v, axis):
        return [shift(v, axis, 1), shift(v, axis, -1)]

    def direct(v, axis):
        return v + shift(v, axis, 1) + shift(v, axis, 2) + shift(v, axis, 3)

    def col_sum(cp):
        return direct(cp + shift(cp, "core", 1), "y")

    lo1, lo3 = both(lo, "y")
    r, cp, w = col_pass(k, direct(rp, "col"), *w)
    w01, w23 = jnp.stack(w[:2]), jnp.stack(w[2:])
    w01_1, w01_3 = both(w01, "col")
    rp, (lo1, lo3) = row_pass(k, col_sum(cp), lo1, lo3)

    hi1, hi3 = both(hi, "y")
    r, cp, (w01_1, w01_3) = col_pass(k, direct(rp, "col"), w01_1, w01_3)
    w23_1, w23_3 = both(w23, "col")
    rp, (lo1, lo3, hi1, hi3) = row_pass(k, col_sum(cp), lo1, lo3, hi1, hi3)

    lo2, hi2 = shift(lo1, "y", 1), shift(hi3, "y", -1)
    k1 = more([lo1, hi1], anchor)
    k3 = more([lo3, hi3], anchor)
    r, cp, (k1, k3, w01_1, w23_1, w01_3, w23_3) = col_pass(k, direct(rp, "col"), k1, k3, w01_1, w23_1, w01_3, w23_3)

    w01_2, w23_2 = shift(w01_1, "col", 1), shift(w23_3, "col", -1)
    k2 = more([lo2, hi2], anchor)
    rs = [r] + [shift(r, "y", s) for s in (1, 2, 3)]
    cp = col_sum(cp)

    place = jnp.stack([core, x]).astype(jnp.int32)
    sib, own = join(place, [w01, w23, w01_1, w23_1, w01_2, w23_2, w01_3, w23_3], [k, k1, k2, k3], rs, cp)
    part = (own + shift(sib, "core", 1).astype(F32)).astype(BF16).reshape(8, 32, COLS)
    return (sum_over_clients(part, z) / CLIENTS).astype(BF16)


def solution(mesh):
    mesh = Mesh(mesh.devices.reshape(8, 4, 2, 4), ("client", "y", "core", "col"))
    row = ("y", "core")
    in_specs = (P("client", "col", row), P(row, "col"), P("client", "col", row))
    out_specs = P(("client", "y", "core"), "col")
    return jax.shard_map(local, mesh=mesh, in_specs=in_specs, out_specs=out_specs, check_vma=False)
```

```python
import functools

import jax
import jax.numpy as jnp
from jax import lax
from jax.experimental import pallas as pl
from jax.experimental.pallas import tpu as pltpu
from jax.sharding import Mesh, PartitionSpec as P

FF = 7168
TOK = 512
ITERS = 3
CLIENTS = 8
entropic = 0.05

F32 = jnp.float32
BF16 = jnp.bfloat16
SIZES = {"client": 8, "y": 4, "core": 2, "col": 4}
ROWS = 896
COLS = 1792
RB = ROWS // 128
CT = 256


def shift(x, axis, s):
    n = SIZES[axis]
    return lax.ppermute(x, axis, [(i, (i + s) % n) for i in range(n)])


def params(mb):
    return pltpu.CompilerParams(vmem_limit_bytes=mb * 1024 * 1024)


VM = pl.BlockSpec(memory_space=pltpu.VMEM)
ANY = pl.BlockSpec(memory_space=pl.ANY)
SMEM = pl.BlockSpec(memory_space=pltpu.SMEM)


def like(v):
    return jax.ShapeDtypeStruct(v.shape, v.dtype)


def block_sums(block):
    return jnp.sum(block.T, axis=0, keepdims=True)


def form_kernel(acts_ref, anchor_ref, k_ref, rp_ref, acc_ref):
    for t in range(COLS // CT):
        sim = lax.dot_general(
            acts_ref[...], anchor_ref[:, t * CT:(t + 1) * CT],
            (((0,), (0,)), ((), ())), preferred_element_type=F32)
        k = jnp.exp(sim * (1.0 / (TOK * entropic)))
        k_ref[:, t * CT:(t + 1) * CT] = k
        part = k[:, :128] + k[:, 128:]
        if t == 0:
            acc_ref[...] = part
        else:
            acc_ref[...] += part
    for b in range(RB):
        rp_ref[pl.ds(b, 1), :] = block_sums(acc_ref[pl.ds(b * 128, 128), :])
    rp_ref[pl.ds(RB, 1), :] = jnp.ones((1, 128), F32)


def first_kernel(place_ref, acts_ref, b_ref, o_ref, m1, m2, m3, pair_ref, sib_ref, k_ref, rp_ref, anchor_ref, acc_ref):
    off = place_ref[0]
    core = place_ref[1]
    half = place_ref[2]

    def put(s, of_core, of_half, value):
        at = lax.rem(s + off, 4) * 128 + 64 * of_core + 32 * of_half
        anchor_ref[pl.ds(pl.multiple_of(at, 32), value.shape[0]), :] = value

    put(0, core, 0, b_ref[...])
    put(0, 1 - core, 0, o_ref[...])
    for s, m in ((1, m1), (2, m2), (3, m3)):
        put(s, core, half, m[pl.ds(64, 32), :])
        put(s, core, 1 - half, pair_ref[s - 1])
        put(s, 1 - core, half, sib_ref[s - 1])
        put(s, 1 - core, 1 - half, sib_ref[s + 2])
    form_kernel(acts_ref, anchor_ref, k_ref, rp_ref, acc_ref)


K_SHAPE = jax.ShapeDtypeStruct((ROWS, COLS), F32)
COST = pl.CostEstimate(flops=2 * TOK * ROWS * COLS, bytes_accessed=10_000_000, transcendentals=ROWS * COLS)


def first(place, acts, b, o, m, pair, sib):
    return pl.pallas_call(
        first_kernel,
        in_specs=[SMEM] + [VM] * 8,
        out_specs=[VM] * 3,
        out_shape=[K_SHAPE, jax.ShapeDtypeStruct((8, 128), F32), jax.ShapeDtypeStruct((TOK, COLS), BF16)],
        scratch_shapes=[pltpu.VMEM((ROWS, 128), F32)],
        compiler_params=params(12),
        cost_estimate=COST,
        name="similarity",
    )(place, acts, b, o, *m, pair, sib)


def more_kernel(n, acts_ref, anchor_ref, *refs):
    k_ref, rp_ref = refs[n:n + 2]
    form_kernel(acts_ref, anchor_ref, k_ref, rp_ref, refs[-1])


def more_halves_kernel(n, lo_ref, hi_ref, anchor_ref, *refs):
    k_ref, rp_ref = refs[n:n + 2]
    acts_ref, acc_ref = refs[-2:]
    acts_ref[pl.ds(0, TOK // 2), :] = lo_ref[...]
    acts_ref[pl.ds(TOK // 2, TOK // 2), :] = hi_ref[...]
    form_kernel(acts_ref, anchor_ref, k_ref, rp_ref, acc_ref)


def more(acts, anchor, *held):
    n = len(held)
    halves = len(acts) == 2
    m = len(acts) + 1
    k, rp, *held = pl.pallas_call(
        functools.partial(more_halves_kernel if halves else more_kernel, n),
        in_specs=[VM] * m + [ANY] * n,
        out_specs=[VM] * 2 + [ANY] * n,
        out_shape=[K_SHAPE, jax.ShapeDtypeStruct((8, 128), F32)] + [like(v) for v in held],
        input_output_aliases={m + i: 2 + i for i in range(n)},
        scratch_shapes=([pltpu.VMEM((TOK, ROWS), BF16)] if halves else []) + [pltpu.VMEM((ROWS, 128), F32)],
        compiler_params=params(12),
        cost_estimate=COST,
        name="more_rows",
    )(*acts, anchor, *held)
    return k, rp, held


def spread(r):
    return jnp.broadcast_to(r, (128, 128)).T


PASS = pl.CostEstimate(flops=8 * ROWS * COLS, bytes_accessed=25_700_000, transcendentals=0)


def col_kernel(k0, k1, k2, k3, p0, p1, p2, p3, r_ref, cp_ref):
    r = (1.0 / FF) / (p0[...] + p1[...] + p2[...] + p3[...])
    r_ref[...] = r
    acc = jnp.zeros((8, COLS), F32)
    for s, k_ref in enumerate((k0, k1, k2, k3)):
        for b in range(RB):
            rb = spread(r[s * 8 + b:s * 8 + b + 1, :])
            for g in range(16):
                scale = jnp.concatenate([rb[8 * g:8 * g + 8, :]] * (COLS // 128), axis=1)
                acc = acc + k_ref[pl.ds(b * 128 + g * 8, 8), :] * scale
    cp_ref[...] = jnp.sum(acc, axis=0, keepdims=True)


def col_pass(ks, parts):
    return pl.pallas_call(
        col_kernel,
        in_specs=[VM] * 8,
        out_specs=[VM] * 2,
        out_shape=[jax.ShapeDtypeStruct((32, 128), F32), jax.ShapeDtypeStruct((1, COLS), F32)],
        compiler_params=params(8),
        cost_estimate=PASS,
        name="column_sums",
    )(*ks, *parts)


def row_kernel(k0, k1, k2, k3, p0, p1, rp_ref, acc_ref, c_ref):
    c_ref[...] = jnp.broadcast_to((1.0 / FF) / (p0[...] + p1[...]), (8, COLS))
    rp_ref[...] = jnp.ones((32, 128), F32)
    for s, k_ref in enumerate((k0, k1, k2, k3)):
        for g in range(ROWS // 64):
            acc = [jnp.zeros((8, 128), F32) for _ in range(8)]
            for t in range(COLS // 128):
                c = c_ref[:, t * 128:(t + 1) * 128]
                for j in range(8):
                    acc[j] = acc[j] + k_ref[pl.ds(64 * g + 8 * j, 8), t * 128:(t + 1) * 128] * c
            for j in range(8):
                acc_ref[pl.ds(64 * g + 8 * j, 8), :] = acc[j]
        for b in range(RB):
            rp_ref[pl.ds(s * 8 + b, 1), :] = block_sums(acc_ref[pl.ds(b * 128, 128), :])


def row_pass(ks, cp, sib):
    return pl.pallas_call(
        row_kernel,
        in_specs=[VM] * 6,
        out_specs=VM,
        out_shape=jax.ShapeDtypeStruct((32, 128), F32),
        scratch_shapes=[pltpu.VMEM((ROWS, 128), F32), pltpu.VMEM((8, COLS), F32)],
        compiler_params=params(8),
        cost_estimate=PASS,
        name="row_sums",
    )(*ks, cp, sib)


def join_kernel(place_ref, w0, w1, wlo, whi, w3, k0, k1, k2, k3, r_ref, c0_ref, c1_ref, sib_ref, own_ref, lhs_ref, rb_ref):
    ks = (k0, k1, k2, k3)
    core = place_ref[0]
    x = place_ref[1]

    @pl.when(pl.program_id(0) == 0)
    def _():
        for s in range(4):
            for b in range(RB):
                rb_ref[pl.ds(s * ROWS + b * 128, 128), :] = spread(r_ref[pl.ds(s * 8 + b, 1), :] * FF)
        for t, w in enumerate((w0, w1, None, w3)):
            at = lax.rem(x + 4 - t, 4) * 64
            for s in range(4):
                if t == 2:
                    src, i = (wlo, s) if s < 2 else (whi, s - 2)
                else:
                    src, i = w, s
                for e in range(2):
                    for h in range(2):
                        half = 1 - core if h == 0 else core
                        lhs_ref[pl.ds(pl.multiple_of(h * 256 + at + e * 32, 32), 32), s * ROWS:(s + 1) * ROWS] = (
                            src[i, pl.ds(pl.multiple_of(32 * half, 32), 32), e * ROWS:(e + 1) * ROWS])

    at = pl.multiple_of(pl.program_id(0) * CT, CT)
    c = (1.0 / FF) / (c0_ref[:, pl.ds(at, CT)] + c1_ref[:, pl.ds(at, CT)])
    total = None
    for s in range(4):
        rb = rb_ref[pl.ds(s * ROWS, ROWS), :]
        k = ks[s][:, pl.ds(at, CT)]
        p = jnp.concatenate(
            [(rb * k[:, h * 128:(h + 1) * 128] * c[:, h * 128:(h + 1) * 128]).astype(BF16) for h in range(CT // 128)], axis=1)
        d = jnp.dot(lhs_ref[:, s * ROWS:(s + 1) * ROWS], p, preferred_element_type=F32)
        total = d if total is None else total + d
    sib_ref[...] = total[:256].astype(BF16)
    own_ref[...] = total[256:]


def join(place, w, ks, r, cp, sib):
    tile = pl.BlockSpec((256, CT), lambda i: (0, i))
    return pl.pallas_call(
        join_kernel,
        grid=(COLS // CT,),
        in_specs=[SMEM] + [VM] * 12,
        out_specs=[tile, tile],
        out_shape=[jax.ShapeDtypeStruct((256, COLS), BF16), jax.ShapeDtypeStruct((256, COLS), F32)],
        scratch_shapes=[pltpu.VMEM((512, 4 * ROWS), BF16), pltpu.VMEM((4 * ROWS, 128), F32)],
        compiler_params=params(14),
        cost_estimate=pl.CostEstimate(flops=2 * 512 * 4 * ROWS * COLS, bytes_accessed=20_000_000, transcendentals=0),
        name="join",
    )(place, *w, *ks, r, cp, sib)


def pick(x, index, axis):
    return lax.dynamic_index_in_dim(x, index, axis, keepdims=False)


def sum_over_clients(part, z):
    def at(s):
        return pick(part, lax.rem(z + 8 + s, 8), 0)

    def wide(v):
        return v.astype(F32)

    far = at(4)
    f1 = shift(far[:16], "client", -2)
    f2 = shift(far[16:], "client", 2)
    u3 = shift(at(-3), "client", -1)
    d3 = shift(at(3), "client", 1)
    u = wide(at(-2)) + wide(u3)
    u = jnp.concatenate([u[:16] + wide(f1), u[16:]], 0).astype(BF16)
    d = wide(at(2)) + wide(d3)
    d = jnp.concatenate([d[:16], d[16:] + wide(f2)], 0).astype(BF16)
    u2 = shift(u, "client", -2)
    d2 = shift(d, "client", 2)
    u1 = shift(at(-1), "client", -1)
    d1 = shift(at(1), "client", 1)
    return wide(at(0)) + wide(u1) + wide(d1) + wide(u2) + wide(d2)


def local(client_acts, anchor_acts, client_weights):
    z = lax.axis_index("client")
    y = lax.axis_index("y")
    core = lax.axis_index("core")
    x = lax.axis_index("col")

    w = client_weights[0].reshape(2, 4, 64, ROWS)
    half = lax.rem(z, 2)
    b_half = lax.dynamic_slice_in_dim(anchor_acts, 32 * half, 32, 0)

    def part(s):
        v = pick(w, lax.rem(y + s, 4), 1)
        return jnp.concatenate([v[0], v[1]], axis=1)

    m = [shift(jnp.concatenate([part(s), b_half], axis=0), "y", s) for s in (1, 2, 3)]
    a = [client_acts[0]] + [shift(client_acts[0], "col", s) for s in (1, 2, 3)]
    o = shift(anchor_acts, "core", 1)
    acts = jnp.concatenate(a, axis=0)

    b_mine = jnp.stack([v[64:] for v in m])
    pair = lax.ppermute(b_mine, "client", [(i, i ^ 1) for i in range(CLIENTS)])
    sib = shift(jnp.concatenate([b_mine, pair], axis=0), "core", 1)

    acts1, acts3 = shift(acts, "y", 1), shift(acts, "y", -1)
    w = jnp.stack([part(0)] + [v[:64] for v in m])
    w1, w3 = shift(w, "col", 1), shift(w, "col", -1)

    place = jnp.stack([lax.rem(x - y + 4, 4), core, half]).astype(jnp.int32)
    k0, p0, anchor = first(place, acts, anchor_acts, o, m, pair, sib)

    lo2, hi2 = shift(acts1[:256], "y", 1), shift(acts3[256:], "y", -1)
    k1, p1, _ = more([acts1], anchor)
    k3, p3, (w1, w3) = more([acts3], anchor, w1, w3)
    lo, hi = shift(w1[:2], "col", 1), shift(w3[2:], "col", -1)
    k2, p2, (lo, hi) = more([lo2, hi2], anchor, lo, hi)

    ks = [k0, k1, k2, k3]
    rp = jnp.concatenate([p0, p1, p2, p3], axis=0)
    for step in range(ITERS):
        r, cp = col_pass(ks, [rp] + [shift(rp, "col", s) for s in (1, 2, 3)])
        sib = shift(cp, "core", 1)
        if step < ITERS - 1:
            rp = row_pass(ks, cp, sib)

    place = jnp.stack([core, x]).astype(jnp.int32)
    sib, own = join(place, [w, w1, lo, hi, w3], ks, r, cp, sib)
    part = (own + shift(sib, "core", 1).astype(F32)).astype(BF16).reshape(8, 32, COLS)
    return (sum_over_clients(part, z) / CLIENTS).astype(BF16)


def solution(mesh):
    mesh = Mesh(mesh.devices.reshape(8, 4, 2, 4), ("client", "y", "core", "col"))
    row = ("y", "core")
    in_specs = (P("client", "col", row), P(row, "col"), P("client", "col", row))
    out_specs = P(("client", "y", "core"), "col")
    return jax.shard_map(local, mesh=mesh, in_specs=in_specs, out_specs=out_specs, check_vma=False)
```

```python
import functools

import jax
import jax.numpy as jnp
from jax import lax
from jax.experimental import pallas as pl
from jax.experimental.pallas import tpu as pltpu
from jax.sharding import Mesh, PartitionSpec as P

FF = 7168
TOK = 512
ITERS = 3
CLIENTS = 8
entropic = 0.05

F32 = jnp.float32
BF16 = jnp.bfloat16
SIZES = {"client": 8, "y": 4, "core": 2, "col": 4}
ROWS = 896
COLS = 1792
RB = ROWS // 128
CT = 256


def shift(x, axis, s):
    n = SIZES[axis]
    return lax.ppermute(x, axis, [(i, (i + s) % n) for i in range(n)])


def params(mb):
    return pltpu.CompilerParams(vmem_limit_bytes=mb * 1024 * 1024)


VM = pl.BlockSpec(memory_space=pltpu.VMEM)
ANY = pl.BlockSpec(memory_space=pl.ANY)
SMEM = pl.BlockSpec(memory_space=pltpu.SMEM)


def like(v):
    return jax.ShapeDtypeStruct(v.shape, v.dtype)


def block_sums(block):
    return jnp.sum(block.T, axis=0, keepdims=True)


def tiles(acts_ref, anchor_ref, k_ref):
    for t in range(COLS // CT):
        sim = lax.dot_general(
            acts_ref[...], anchor_ref[:, t * CT:(t + 1) * CT],
            (((0,), (0,)), ((), ())), preferred_element_type=F32)
        k = jnp.exp(sim * (1.0 / (TOK * entropic)))
        k_ref[:, t * CT:(t + 1) * CT] = k
        yield t, k


def first_kernel(n, place_ref, acts_ref, b_ref, m1, m2, m3, pair_ref, sib_ref, *refs):
    k_ref, rp_ref, anchor_ref = refs[n:n + 3]
    acc_ref = refs[-1]
    off = place_ref[0]
    core = place_ref[1]
    half = place_ref[2]

    def put(s, of_core, of_half, value):
        at = lax.rem(s + off, 4) * 128 + 64 * of_core + 32 * of_half
        anchor_ref[pl.ds(pl.multiple_of(at, 32), value.shape[0]), :] = value

    put(0, core, 0, b_ref[...])
    put(0, 1 - core, 0, sib_ref[0])
    put(0, 1 - core, 1, sib_ref[1])
    for s, m in ((1, m1), (2, m2), (3, m3)):
        put(s, core, half, m[pl.ds(64, 32), :])
        put(s, core, 1 - half, pair_ref[s - 1])
        put(s, 1 - core, half, sib_ref[s + 1])
        put(s, 1 - core, 1 - half, sib_ref[s + 4])
    row_partials(acts_ref, anchor_ref, k_ref, rp_ref, acc_ref)


def row_partials(acts_ref, anchor_ref, k_ref, rp_ref, acc_ref):
    for t, k in tiles(acts_ref, anchor_ref, k_ref):
        part = k[:, :128] + k[:, 128:]
        if t == 0:
            acc_ref[...] = part
        else:
            acc_ref[...] += part
    for b in range(RB):
        rp_ref[pl.ds(b, 1), :] = block_sums(acc_ref[pl.ds(b * 128, 128), :])
    rp_ref[pl.ds(RB, 1), :] = jnp.ones((1, 128), F32)


K_SHAPE = jax.ShapeDtypeStruct((ROWS, COLS), F32)
COST = pl.CostEstimate(flops=2 * TOK * ROWS * COLS, bytes_accessed=10_000_000, transcendentals=ROWS * COLS)


def first(place, acts, b, m, pair, sib, *held):
    n = len(held)
    k, rp, anchor, *held = pl.pallas_call(
        functools.partial(first_kernel, n),
        in_specs=[SMEM] + [VM] * 7 + [ANY] * n,
        out_specs=[VM] * 3 + [ANY] * n,
        out_shape=[K_SHAPE, jax.ShapeDtypeStruct((8, 128), F32), jax.ShapeDtypeStruct((TOK, COLS), BF16)] + [like(v) for v in held],
        input_output_aliases={8 + i: 3 + i for i in range(n)},
        scratch_shapes=[pltpu.VMEM((ROWS, 128), F32)],
        compiler_params=params(8),
        cost_estimate=COST,
        name="similarity",
    )(place, acts, b, *m, pair, sib, *held)
    return k, rp, anchor, held


def spread(r):
    return jnp.broadcast_to(r, (128, 128)).T


def more_kernel(n, acts_ref, anchor_ref, *refs):
    k_ref, rp_ref = refs[n:n + 2]
    row_partials(acts_ref, anchor_ref, k_ref, rp_ref, refs[-1])


def more_halves_kernel(n, lo_ref, hi_ref, anchor_ref, *refs):
    k_ref, rp_ref = refs[n:n + 2]
    acts_ref, acc_ref = refs[-2:]
    acts_ref[pl.ds(0, TOK // 2), :] = lo_ref[...]
    acts_ref[pl.ds(TOK // 2, TOK // 2), :] = hi_ref[...]
    row_partials(acts_ref, anchor_ref, k_ref, rp_ref, acc_ref)


def more(acts, anchor, *held):
    n = len(held)
    halves = len(acts) == 2
    m = len(acts) + 1
    k, rp, *held = pl.pallas_call(
        functools.partial(more_halves_kernel if halves else more_kernel, n),
        in_specs=[VM] * m + [ANY] * n,
        out_specs=[VM] * 2 + [ANY] * n,
        out_shape=[K_SHAPE, jax.ShapeDtypeStruct((8, 128), F32)] + [like(v) for v in held],
        input_output_aliases={m + i: 2 + i for i in range(n)},
        scratch_shapes=([pltpu.VMEM((TOK, ROWS), BF16)] if halves else []) + [pltpu.VMEM((ROWS, 128), F32)],
        compiler_params=params(8),
        cost_estimate=COST,
        name="more_rows",
    )(*acts, anchor, *held)
    return k, rp, held


def add_rows(acc, k_ref, r):
    for b in range(RB):
        rb = spread(r[b:b + 1, :])
        for g in range(16):
            scale = jnp.concatenate([rb[8 * g:8 * g + 8, :]] * (COLS // 128), axis=1)
            acc = acc + k_ref[pl.ds(b * 128 + g * 8, 8), :] * scale
    return acc


PASS = pl.CostEstimate(flops=8 * ROWS * COLS, bytes_accessed=25_700_000, transcendentals=0)


def col_kernel(n, k0, k1, k2, k3, p0, p1, p2, p3, *refs):
    r_ref, cp_ref = refs[n:n + 2]
    r = (1.0 / FF) / (p0[...] + p1[...] + p2[...] + p3[...])
    r_ref[...] = r
    acc = jnp.zeros((8, COLS), F32)
    for s, k_ref in enumerate((k0, k1, k2, k3)):
        acc = add_rows(acc, k_ref, r[8 * s:8 * s + 8, :])
    cp_ref[...] = jnp.sum(acc, axis=0, keepdims=True)


def col_pass(ks, parts, *held):
    n = len(held)
    r, cp, *held = pl.pallas_call(
        functools.partial(col_kernel, n),
        in_specs=[VM] * 8 + [ANY] * n,
        out_specs=[VM] * 2 + [ANY] * n,
        out_shape=[jax.ShapeDtypeStruct((32, 128), F32), jax.ShapeDtypeStruct((1, COLS), F32)] + [like(v) for v in held],
        input_output_aliases={8 + i: 2 + i for i in range(n)},
        compiler_params=params(4),
        cost_estimate=PASS,
        name="column_sums",
    )(*ks, *parts, *held)
    return r, cp, held


def row_kernel(k0, k1, k2, k3, p0, p1, rp_ref, acc_ref, c_ref):
    c_ref[...] = jnp.broadcast_to((1.0 / FF) / (p0[...] + p1[...]), (8, COLS))
    rp_ref[...] = jnp.ones((32, 128), F32)
    for s, k_ref in enumerate((k0, k1, k2, k3)):
        for g in range(ROWS // 64):
            acc = [jnp.zeros((8, 128), F32) for _ in range(8)]
            for t in range(COLS // 128):
                c = c_ref[:, t * 128:(t + 1) * 128]
                for j in range(8):
                    acc[j] = acc[j] + k_ref[pl.ds(64 * g + 8 * j, 8), t * 128:(t + 1) * 128] * c
            for j in range(8):
                acc_ref[pl.ds(64 * g + 8 * j, 8), :] = acc[j]
        for b in range(RB):
            rp_ref[pl.ds(s * 8 + b, 1), :] = block_sums(acc_ref[pl.ds(b * 128, 128), :])


def row_pass(ks, cp, sib):
    return pl.pallas_call(
        row_kernel,
        in_specs=[VM] * 6,
        out_specs=VM,
        out_shape=jax.ShapeDtypeStruct((32, 128), F32),
        scratch_shapes=[pltpu.VMEM((ROWS, 128), F32), pltpu.VMEM((8, COLS), F32)],
        compiler_params=params(4),
        cost_estimate=PASS,
        name="row_sums",
    )(*ks, cp, sib)


def join_kernel(place_ref, w0, w1, wlo, whi, w3, k0, k1, k2, k3, r_ref, c0_ref, c1_ref, sib_ref, own_ref, lhs_ref, rb_ref):
    ks = (k0, k1, k2, k3)
    core = place_ref[0]
    x = place_ref[1]

    @pl.when(pl.program_id(0) == 0)
    def _():
        for s in range(4):
            for b in range(RB):
                rb_ref[pl.ds(s * ROWS + b * 128, 128), :] = spread(r_ref[pl.ds(s * 8 + b, 1), :] * FF)
        for t, w in enumerate((w0, w1, None, w3)):
            at = lax.rem(x + 4 - t, 4) * 64
            for s in range(4):
                src, i = ((wlo, whi)[s // 2], s % 2) if t == 2 else (w, s)
                for e in range(2):
                    for h in range(2):
                        half = 1 - core if h == 0 else core
                        lhs_ref[pl.ds(pl.multiple_of(h * 256 + at + e * 32, 32), 32), s * ROWS:(s + 1) * ROWS] = (
                            src[i, pl.ds(pl.multiple_of(32 * half, 32), 32), e * ROWS:(e + 1) * ROWS])

    at = pl.multiple_of(pl.program_id(0) * CT, CT)
    c = (1.0 / FF) / (c0_ref[:, pl.ds(at, CT)] + c1_ref[:, pl.ds(at, CT)])
    total = None
    for s in range(4):
        rb = rb_ref[pl.ds(s * ROWS, ROWS), :]
        k = ks[s][:, pl.ds(at, CT)]
        p = jnp.concatenate(
            [(rb * k[:, h * 128:(h + 1) * 128] * c[:, h * 128:(h + 1) * 128]).astype(BF16) for h in range(CT // 128)], axis=1)
        d = jnp.dot(lhs_ref[:, s * ROWS:(s + 1) * ROWS], p, preferred_element_type=F32)
        total = d if total is None else total + d
    sib_ref[:, pl.ds(at, CT)] = total[:256].astype(BF16)
    own_ref[:, pl.ds(at, CT)] = total[256:]


def join(place, w, ks, r, cp, sib):
    return pl.pallas_call(
        join_kernel,
        grid=(COLS // CT,),
        in_specs=[SMEM] + [VM] * 12,
        out_specs=[VM, VM],
        out_shape=[jax.ShapeDtypeStruct((256, COLS), BF16), jax.ShapeDtypeStruct((256, COLS), F32)],
        scratch_shapes=[pltpu.VMEM((512, 4 * ROWS), BF16), pltpu.VMEM((4 * ROWS, 128), F32)],
        compiler_params=params(9),
        cost_estimate=pl.CostEstimate(flops=2 * 512 * 4 * ROWS * COLS, bytes_accessed=20_000_000, transcendentals=0),
        name="join",
    )(place, *w, *ks, r, cp, sib)


def pick(x, index, axis):
    return lax.dynamic_index_in_dim(x, index, axis, keepdims=False)


def sum_over_clients(part, z):
    def at(s):
        return pick(part, lax.rem(z + 8 + s, 8), 0)

    def wide(v):
        return v.astype(F32)

    far = at(4)
    f1 = shift(far[:16], "client", -2)
    f2 = shift(far[16:], "client", 2)
    u3 = shift(at(-3), "client", -1)
    d3 = shift(at(3), "client", 1)
    u = wide(at(-2)) + wide(u3)
    u = jnp.concatenate([u[:16] + wide(f1), u[16:]], 0).astype(BF16)
    d = wide(at(2)) + wide(d3)
    d = jnp.concatenate([d[:16], d[16:] + wide(f2)], 0).astype(BF16)
    u2 = shift(u, "client", -2)
    d2 = shift(d, "client", 2)
    u1 = shift(at(-1), "client", -1)
    d1 = shift(at(1), "client", 1)
    return wide(at(0)) + wide(u1) + wide(d1) + wide(u2) + wide(d2)


def local(client_acts, anchor_acts, client_weights):
    z = lax.axis_index("client")
    y = lax.axis_index("y")
    core = lax.axis_index("core")
    x = lax.axis_index("col")

    w = client_weights[0].reshape(2, 4, 64, ROWS)
    half = lax.rem(z, 2)
    b_half = lax.dynamic_slice_in_dim(anchor_acts, 32 * half, 32, 0)

    def part(s):
        v = pick(w, lax.rem(y + s, 4), 1)
        return jnp.concatenate([v[0], v[1]], axis=1)

    m = [shift(jnp.concatenate([part(s), b_half], axis=0), "y", s) for s in (1, 2, 3)]
    a = [client_acts[0]] + [shift(client_acts[0], "col", s) for s in (1, 2, 3)]
    acts = jnp.concatenate(a, axis=0)

    b_mine = jnp.stack([v[64:] for v in m])
    pair = lax.ppermute(b_mine, "client", [(i, i ^ 1) for i in range(CLIENTS)])
    sib = shift(jnp.concatenate([anchor_acts.reshape(2, 32, COLS), b_mine, pair], axis=0), "core", 1)

    acts1, acts3 = shift(acts, "y", 1), shift(acts, "y", -1)
    lo2, hi2 = shift(acts1[:256], "y", 1), shift(acts3[256:], "y", -1)

    w = jnp.stack([part(0)] + [v[:64] for v in m])
    place = jnp.stack([lax.rem(x - y + 4, 4), core, half]).astype(jnp.int32)
    w1, w3 = shift(w, "col", 1), shift(w, "col", -1)
    k0, p0, anchor, _ = first(place, acts, anchor_acts, m, pair, sib)

    k1, p1, _ = more([acts1], anchor)
    k3, p3, (w1, w3) = more([acts3], anchor, w1, w3)
    w2 = [shift(w1[:2], "col", 1), shift(w3[2:], "col", -1)]
    k2, p2, _ = more([lo2, hi2], anchor)
    ks = [k0, k1, k2, k3]
    rp = jnp.concatenate([p0, p1, p2, p3], axis=0)

    for step in range(ITERS):
        r, cp, w2 = col_pass(ks, [rp] + [shift(rp, "col", s) for s in (1, 2, 3)], *w2)
        sib = shift(cp, "core", 1)
        if step < ITERS - 1:
            rp = row_pass(ks, cp, sib)

    place = jnp.stack([core, x]).astype(jnp.int32)
    sib, own = join(place, [w, w1, *w2, w3], ks, r, cp, sib)
    part = (own + shift(sib, "core", 1).astype(F32)).astype(BF16).reshape(8, 32, COLS)
    return (sum_over_clients(part, z) / CLIENTS).astype(BF16)


def solution(mesh):
    mesh = Mesh(mesh.devices.reshape(8, 4, 2, 4), ("client", "y", "core", "col"))
    row = ("y", "core")
    in_specs = (P("client", "col", row), P(row, "col"), P("client", "col", row))
    out_specs = P(("client", "y", "core"), "col")
    return jax.shard_map(local, mesh=mesh, in_specs=in_specs, out_specs=out_specs, check_vma=False)
```

```python
import functools

import jax
import jax.numpy as jnp
from jax import lax
from jax.experimental import pallas as pl
from jax.experimental.pallas import tpu as pltpu
from jax.sharding import Mesh, PartitionSpec as P

FF = 7168
TOK = 512
ITERS = 3
CLIENTS = 8
entropic = 0.05

F32 = jnp.float32
BF16 = jnp.bfloat16
SIZES = {"client": 8, "y": 4, "core": 2, "col": 4}
ROWS = 896
COLS = 1792
RB = ROWS // 128
CT = 256


def shift(x, axis, s):
    n = SIZES[axis]
    return lax.ppermute(x, axis, [(i, (i + s) % n) for i in range(n)])


def params(mb):
    return pltpu.CompilerParams(vmem_limit_bytes=mb * 1024 * 1024)


VM = pl.BlockSpec(memory_space=pltpu.VMEM)
ANY = pl.BlockSpec(memory_space=pl.ANY)
SMEM = pl.BlockSpec(memory_space=pltpu.SMEM)


def like(v):
    return jax.ShapeDtypeStruct(v.shape, v.dtype)


def block_sums(block):
    return jnp.sum(block.T, axis=0, keepdims=True)


def tiles(acts_ref, anchor_ref, k_ref):
    for t in range(COLS // CT):
        sim = lax.dot_general(
            acts_ref[...], anchor_ref[:, t * CT:(t + 1) * CT],
            (((0,), (0,)), ((), ())), preferred_element_type=F32)
        k = jnp.exp(sim * (1.0 / (TOK * entropic)))
        k_ref[:, t * CT:(t + 1) * CT] = k
        yield t, k


def first_kernel(n, place_ref, acts_ref, b_ref, m1, m2, m3, pair_ref, sib_ref, *refs):
    k_ref, rp_ref, anchor_ref = refs[n:n + 3]
    acc_ref = refs[-1]
    off = place_ref[0]
    core = place_ref[1]
    half = place_ref[2]

    def put(s, of_core, of_half, value):
        at = lax.rem(s + off, 4) * 128 + 64 * of_core + 32 * of_half
        anchor_ref[pl.ds(pl.multiple_of(at, 32), value.shape[0]), :] = value

    put(0, core, 0, b_ref[...])
    put(0, 1 - core, 0, sib_ref[0])
    put(0, 1 - core, 1, sib_ref[1])
    for s, m in ((1, m1), (2, m2), (3, m3)):
        put(s, core, half, m[pl.ds(64, 32), :])
        put(s, core, 1 - half, pair_ref[s - 1])
        put(s, 1 - core, half, sib_ref[s + 1])
        put(s, 1 - core, 1 - half, sib_ref[s + 4])
    row_partials(acts_ref, anchor_ref, k_ref, rp_ref, acc_ref)


def row_partials(acts_ref, anchor_ref, k_ref, rp_ref, acc_ref):
    for t, k in tiles(acts_ref, anchor_ref, k_ref):
        part = k[:, :128] + k[:, 128:]
        if t == 0:
            acc_ref[...] = part
        else:
            acc_ref[...] += part
    for b in range(RB):
        rp_ref[pl.ds(b, 1), :] = block_sums(acc_ref[pl.ds(b * 128, 128), :])
    rp_ref[pl.ds(RB, 1), :] = jnp.ones((1, 128), F32)


K_SHAPE = jax.ShapeDtypeStruct((ROWS, COLS), F32)
COST = pl.CostEstimate(flops=2 * TOK * ROWS * COLS, bytes_accessed=10_000_000, transcendentals=ROWS * COLS)


def first(place, acts, b, m, pair, sib, *held):
    n = len(held)
    k, rp, anchor, *held = pl.pallas_call(
        functools.partial(first_kernel, n),
        in_specs=[SMEM] + [VM] * 7 + [ANY] * n,
        out_specs=[VM] * 3 + [ANY] * n,
        out_shape=[K_SHAPE, jax.ShapeDtypeStruct((8, 128), F32), jax.ShapeDtypeStruct((TOK, COLS), BF16)] + [like(v) for v in held],
        input_output_aliases={8 + i: 3 + i for i in range(n)},
        scratch_shapes=[pltpu.VMEM((ROWS, 128), F32)],
        compiler_params=params(12),
        cost_estimate=COST,
        name="similarity",
    )(place, acts, b, *m, pair, sib, *held)
    return k, rp, anchor, held


def spread(r):
    return jnp.broadcast_to(r, (128, 128)).T


def more_kernel(n, acts_ref, anchor_ref, *refs):
    k_ref, rp_ref = refs[n:n + 2]
    row_partials(acts_ref, anchor_ref, k_ref, rp_ref, refs[-1])


def more_halves_kernel(n, lo_ref, hi_ref, anchor_ref, *refs):
    k_ref, rp_ref = refs[n:n + 2]
    acts_ref, acc_ref = refs[-2:]
    acts_ref[pl.ds(0, TOK // 2), :] = lo_ref[...]
    acts_ref[pl.ds(TOK // 2, TOK // 2), :] = hi_ref[...]
    row_partials(acts_ref, anchor_ref, k_ref, rp_ref, acc_ref)


def more(acts, anchor, *held):
    n = len(held)
    halves = len(acts) == 2
    m = len(acts) + 1
    k, rp, *held = pl.pallas_call(
        functools.partial(more_halves_kernel if halves else more_kernel, n),
        in_specs=[VM] * m + [ANY] * n,
        out_specs=[VM] * 2 + [ANY] * n,
        out_shape=[K_SHAPE, jax.ShapeDtypeStruct((8, 128), F32)] + [like(v) for v in held],
        input_output_aliases={m + i: 2 + i for i in range(n)},
        scratch_shapes=([pltpu.VMEM((TOK, ROWS), BF16)] if halves else []) + [pltpu.VMEM((ROWS, 128), F32)],
        compiler_params=params(12),
        cost_estimate=COST,
        name="more_rows",
    )(*acts, anchor, *held)
    return k, rp, held


def add_rows(acc, k_ref, r):
    for b in range(RB):
        rb = spread(r[b:b + 1, :])
        for g in range(16):
            scale = jnp.concatenate([rb[8 * g:8 * g + 8, :]] * (COLS // 128), axis=1)
            acc = acc + k_ref[pl.ds(b * 128 + g * 8, 8), :] * scale
    return acc


PASS = pl.CostEstimate(flops=8 * ROWS * COLS, bytes_accessed=25_700_000, transcendentals=0)


def col_kernel(n, k0, k1, k2, k3, p0, p1, p2, p3, *refs):
    r_ref, cp_ref = refs[n:n + 2]
    r = (1.0 / FF) / (p0[...] + p1[...] + p2[...] + p3[...])
    r_ref[...] = r
    acc = jnp.zeros((8, COLS), F32)
    for s, k_ref in enumerate((k0, k1, k2, k3)):
        acc = add_rows(acc, k_ref, r[8 * s:8 * s + 8, :])
    cp_ref[...] = jnp.sum(acc, axis=0, keepdims=True)


def col_pass(ks, parts, *held):
    n = len(held)
    r, cp, *held = pl.pallas_call(
        functools.partial(col_kernel, n),
        in_specs=[VM] * 8 + [ANY] * n,
        out_specs=[VM] * 2 + [ANY] * n,
        out_shape=[jax.ShapeDtypeStruct((32, 128), F32), jax.ShapeDtypeStruct((1, COLS), F32)] + [like(v) for v in held],
        input_output_aliases={8 + i: 2 + i for i in range(n)},
        compiler_params=params(12),
        cost_estimate=PASS,
        name="column_sums",
    )(*ks, *parts, *held)
    return r, cp, held


def row_kernel(k0, k1, k2, k3, p0, p1, rp_ref, acc_ref, c_ref):
    c_ref[...] = jnp.broadcast_to((1.0 / FF) / (p0[...] + p1[...]), (8, COLS))
    rp_ref[...] = jnp.ones((32, 128), F32)
    for s, k_ref in enumerate((k0, k1, k2, k3)):
        for g in range(ROWS // 64):
            acc = [jnp.zeros((8, 128), F32) for _ in range(8)]
            for t in range(COLS // 128):
                c = c_ref[:, t * 128:(t + 1) * 128]
                for j in range(8):
                    acc[j] = acc[j] + k_ref[pl.ds(64 * g + 8 * j, 8), t * 128:(t + 1) * 128] * c
            for j in range(8):
                acc_ref[pl.ds(64 * g + 8 * j, 8), :] = acc[j]
        for b in range(RB):
            rp_ref[pl.ds(s * 8 + b, 1), :] = block_sums(acc_ref[pl.ds(b * 128, 128), :])


def row_pass(ks, cp, sib):
    return pl.pallas_call(
        row_kernel,
        in_specs=[VM] * 6,
        out_specs=VM,
        out_shape=jax.ShapeDtypeStruct((32, 128), F32),
        scratch_shapes=[pltpu.VMEM((ROWS, 128), F32), pltpu.VMEM((8, COLS), F32)],
        compiler_params=params(12),
        cost_estimate=PASS,
        name="row_sums",
    )(*ks, cp, sib)


def join_kernel(place_ref, w0, w1, wlo, whi, w3, k0, k1, k2, k3, r_ref, c0_ref, c1_ref, sib_ref, own_ref, lhs_ref, rb_ref):
    ks = (k0, k1, k2, k3)
    core = place_ref[0]
    x = place_ref[1]

    @pl.when(pl.program_id(0) == 0)
    def _():
        for s in range(4):
            for b in range(RB):
                rb_ref[pl.ds(s * ROWS + b * 128, 128), :] = spread(r_ref[pl.ds(s * 8 + b, 1), :] * FF)
        for t, w in enumerate((w0, w1, None, w3)):
            at = lax.rem(x + 4 - t, 4) * 64
            for s in range(4):
                src, i = ((wlo, whi)[s // 2], s % 2) if t == 2 else (w, s)
                for e in range(2):
                    for h in range(2):
                        half = 1 - core if h == 0 else core
                        lhs_ref[pl.ds(pl.multiple_of(h * 256 + at + e * 32, 32), 32), s * ROWS:(s + 1) * ROWS] = (
                            src[i, pl.ds(pl.multiple_of(32 * half, 32), 32), e * ROWS:(e + 1) * ROWS])

    at = pl.multiple_of(pl.program_id(0) * CT, CT)
    c = (1.0 / FF) / (c0_ref[:, pl.ds(at, CT)] + c1_ref[:, pl.ds(at, CT)])
    total = None
    for s in range(4):
        rb = rb_ref[pl.ds(s * ROWS, ROWS), :]
        k = ks[s][:, pl.ds(at, CT)]
        p = jnp.concatenate(
            [(rb * k[:, h * 128:(h + 1) * 128] * c[:, h * 128:(h + 1) * 128]).astype(BF16) for h in range(CT // 128)], axis=1)
        d = jnp.dot(lhs_ref[:, s * ROWS:(s + 1) * ROWS], p, preferred_element_type=F32)
        total = d if total is None else total + d
    sib_ref[:, pl.ds(at, CT)] = total[:256].astype(BF16)
    own_ref[:, pl.ds(at, CT)] = total[256:].astype(BF16)


def join(place, w, ks, r, cp, sib):
    return pl.pallas_call(
        join_kernel,
        grid=(COLS // CT,),
        in_specs=[SMEM] + [VM] * 12,
        out_specs=[VM, VM],
        out_shape=[jax.ShapeDtypeStruct((256, COLS), BF16)] * 2,
        scratch_shapes=[pltpu.VMEM((512, 4 * ROWS), BF16), pltpu.VMEM((4 * ROWS, 128), F32)],
        compiler_params=params(12),
        cost_estimate=pl.CostEstimate(flops=2 * 512 * 4 * ROWS * COLS, bytes_accessed=20_000_000, transcendentals=0),
        name="join",
    )(place, *w, *ks, r, cp, sib)


def add_kernel(own_ref, other_ref, out_ref):
    out_ref[0] = (own_ref[...].astype(F32) + other_ref[...].astype(F32)).astype(BF16)


def add(own, other):
    tile = pl.BlockSpec((32, COLS), lambda i: (i, 0))
    return pl.pallas_call(
        add_kernel,
        grid=(CLIENTS,),
        in_specs=[tile] * 2,
        out_specs=pl.BlockSpec((1, 32, COLS), lambda i: (i, 0, 0)),
        out_shape=jax.ShapeDtypeStruct((CLIENTS, 32, COLS), BF16),
        compiler_params=params(12),
        cost_estimate=pl.CostEstimate(flops=256 * COLS, bytes_accessed=2_800_000, transcendentals=0),
        name="add_cores",
    )(own, other)


def pick(x, index, axis):
    return lax.dynamic_index_in_dim(x, index, axis, keepdims=False)


def sum_over_clients(part, z):
    def at(s):
        return pick(part, lax.rem(z + 8 + s, 8), 0)

    def wide(v):
        return v.astype(F32)

    far = at(4)
    f1 = shift(far[:16], "client", -2)
    f2 = shift(far[16:], "client", 2)
    u3 = shift(at(-3), "client", -1)
    d3 = shift(at(3), "client", 1)
    u = wide(at(-2)) + wide(u3)
    u = jnp.concatenate([u[:16] + wide(f1), u[16:]], 0).astype(BF16)
    d = wide(at(2)) + wide(d3)
    d = jnp.concatenate([d[:16], d[16:] + wide(f2)], 0).astype(BF16)
    u2 = shift(u, "client", -2)
    d2 = shift(d, "client", 2)
    u1 = shift(at(-1), "client", -1)
    d1 = shift(at(1), "client", 1)
    return wide(at(0)) + wide(u1) + wide(d1) + wide(u2) + wide(d2)


def local(client_acts, anchor_acts, client_weights):
    z = lax.axis_index("client")
    y = lax.axis_index("y")
    core = lax.axis_index("core")
    x = lax.axis_index("col")

    w = client_weights[0].reshape(2, 4, 64, ROWS)
    half = lax.rem(z, 2)
    b_half = lax.dynamic_slice_in_dim(anchor_acts, 32 * half, 32, 0)

    def part(s):
        v = pick(w, lax.rem(y + s, 4), 1)
        return jnp.concatenate([v[0], v[1]], axis=1)

    m = [shift(jnp.concatenate([part(s), b_half], axis=0), "y", s) for s in (1, 2, 3)]
    a = [client_acts[0]] + [shift(client_acts[0], "col", s) for s in (1, 2, 3)]
    acts = jnp.concatenate(a, axis=0)

    b_mine = jnp.stack([v[64:] for v in m])
    pair = lax.ppermute(b_mine, "client", [(i, i ^ 1) for i in range(CLIENTS)])
    sib = shift(jnp.concatenate([anchor_acts.reshape(2, 32, COLS), b_mine, pair], axis=0), "core", 1)

    acts1, acts3 = shift(acts, "y", 1), shift(acts, "y", -1)
    lo2, hi2 = shift(acts1[:256], "y", 1), shift(acts3[256:], "y", -1)

    w = jnp.stack([part(0)] + [v[:64] for v in m])
    place = jnp.stack([lax.rem(x - y + 4, 4), core, half]).astype(jnp.int32)
    w1, w3 = shift(w, "col", 1), shift(w, "col", -1)
    k0, p0, anchor, (w1, w3) = first(place, acts, anchor_acts, m, pair, sib, w1, w3)
    w2 = [shift(w1[:2], "col", 1), shift(w3[2:], "col", -1)]

    k1, p1, _ = more([acts1], anchor)
    k3, p3, _ = more([acts3], anchor)
    k2, p2, _ = more([lo2, hi2], anchor)
    ks = [k0, k1, k2, k3]
    rp = jnp.concatenate([p0, p1, p2, p3], axis=0)

    for step in range(ITERS):
        held = w2 if step == 0 else []
        r, cp, held = col_pass(ks, [rp] + [shift(rp, "col", s) for s in (1, 2, 3)], *held)
        w2 = held if step == 0 else w2
        sib = shift(cp, "core", 1)
        if step < ITERS - 1:
            rp = row_pass(ks, cp, sib)

    place = jnp.stack([core, x]).astype(jnp.int32)
    sib, own = join(place, [w, w1, *w2, w3], ks, r, cp, sib)
    part = add(own, shift(sib, "core", 1))
    return (sum_over_clients(part, z) / CLIENTS).astype(BF16)


def solution(mesh):
    mesh = Mesh(mesh.devices.reshape(8, 4, 2, 4), ("client", "y", "core", "col"))
    row = ("y", "core")
    in_specs = (P("client", "col", row), P(row, "col"), P("client", "col", row))
    out_specs = P(("client", "y", "core"), "col")
    return jax.shard_map(local, mesh=mesh, in_specs=in_specs, out_specs=out_specs, check_vma=False)
```

```python
import functools

import jax
import jax.numpy as jnp
from jax import lax
from jax.experimental import pallas as pl
from jax.experimental.pallas import tpu as pltpu
from jax.sharding import Mesh, PartitionSpec as P

FF = 7168
TOK = 512
ITERS = 3
CLIENTS = 8
entropic = 0.05

F32 = jnp.float32
BF16 = jnp.bfloat16
SIZES = {"client": 8, "y": 4, "core": 2, "col": 4}
ROWS = 896
COLS = 1792
RB = ROWS // 128
CT = 256


def shift(x, axis, s):
    n = SIZES[axis]
    return lax.ppermute(x, axis, [(i, (i + s) % n) for i in range(n)])


def params(mb):
    return pltpu.CompilerParams(vmem_limit_bytes=mb * 1024 * 1024)


VM = pl.BlockSpec(memory_space=pltpu.VMEM)
ANY = pl.BlockSpec(memory_space=pl.ANY)
SMEM = pl.BlockSpec(memory_space=pltpu.SMEM)


def like(v):
    return jax.ShapeDtypeStruct(v.shape, v.dtype)


def block_sums(block):
    return jnp.sum(block.T, axis=0, keepdims=True)


def tiles(acts_ref, anchor_ref, k_ref):
    for t in range(COLS // CT):
        sim = lax.dot_general(
            acts_ref[...], anchor_ref[:, t * CT:(t + 1) * CT],
            (((0,), (0,)), ((), ())), preferred_element_type=F32)
        k = jnp.exp(sim * (1.0 / (TOK * entropic)))
        k_ref[:, t * CT:(t + 1) * CT] = k
        yield t, k


def first_kernel(n, place_ref, acts_ref, b_ref, m1, m2, m3, pair_ref, sib_ref, *refs):
    k_ref, rp_ref, anchor_ref = refs[n:n + 3]
    acc_ref = refs[-1]
    off = place_ref[0]
    core = place_ref[1]
    half = place_ref[2]

    def put(s, of_core, of_half, value):
        at = lax.rem(s + off, 4) * 128 + 64 * of_core + 32 * of_half
        anchor_ref[pl.ds(pl.multiple_of(at, 32), value.shape[0]), :] = value

    put(0, core, 0, b_ref[...])
    put(0, 1 - core, 0, sib_ref[0])
    put(0, 1 - core, 1, sib_ref[1])
    for s, m in ((1, m1), (2, m2), (3, m3)):
        put(s, core, half, m[pl.ds(64, 32), :])
        put(s, core, 1 - half, pair_ref[s - 1])
        put(s, 1 - core, half, sib_ref[s + 1])
        put(s, 1 - core, 1 - half, sib_ref[s + 4])
    row_partials(acts_ref, anchor_ref, k_ref, rp_ref, acc_ref)


def row_partials(acts_ref, anchor_ref, k_ref, rp_ref, acc_ref):
    for t, k in tiles(acts_ref, anchor_ref, k_ref):
        part = k[:, :128] + k[:, 128:]
        if t == 0:
            acc_ref[...] = part
        else:
            acc_ref[...] += part
    for b in range(RB):
        rp_ref[pl.ds(b, 1), :] = block_sums(acc_ref[pl.ds(b * 128, 128), :])
    rp_ref[pl.ds(RB, 1), :] = jnp.ones((1, 128), F32)


K_SHAPE = jax.ShapeDtypeStruct((ROWS, COLS), F32)
COST = pl.CostEstimate(flops=2 * TOK * ROWS * COLS, bytes_accessed=10_000_000, transcendentals=ROWS * COLS)


def first(place, acts, b, m, pair, sib, *held):
    n = len(held)
    k, rp, anchor, *held = pl.pallas_call(
        functools.partial(first_kernel, n),
        in_specs=[SMEM] + [VM] * 7 + [ANY] * n,
        out_specs=[VM] * 3 + [ANY] * n,
        out_shape=[K_SHAPE, jax.ShapeDtypeStruct((8, 128), F32), jax.ShapeDtypeStruct((TOK, COLS), BF16)] + [like(v) for v in held],
        input_output_aliases={8 + i: 3 + i for i in range(n)},
        scratch_shapes=[pltpu.VMEM((ROWS, 128), F32)],
        compiler_params=params(12),
        cost_estimate=COST,
        name="similarity",
    )(place, acts, b, *m, pair, sib, *held)
    return k, rp, anchor, held


def spread(r):
    return jnp.broadcast_to(r, (128, 128)).T


def more_kernel(n, acts_ref, anchor_ref, *refs):
    k_ref, rp_ref = refs[n:n + 2]
    row_partials(acts_ref, anchor_ref, k_ref, rp_ref, refs[-1])


def more_halves_kernel(n, lo_ref, hi_ref, anchor_ref, *refs):
    k_ref, rp_ref = refs[n:n + 2]
    acts_ref, acc_ref = refs[-2:]
    acts_ref[pl.ds(0, TOK // 2), :] = lo_ref[...]
    acts_ref[pl.ds(TOK // 2, TOK // 2), :] = hi_ref[...]
    row_partials(acts_ref, anchor_ref, k_ref, rp_ref, acc_ref)


def more(acts, anchor, *held):
    n = len(held)
    halves = len(acts) == 2
    m = len(acts) + 1
    k, rp, *held = pl.pallas_call(
        functools.partial(more_halves_kernel if halves else more_kernel, n),
        in_specs=[VM] * m + [ANY] * n,
        out_specs=[VM] * 2 + [ANY] * n,
        out_shape=[K_SHAPE, jax.ShapeDtypeStruct((8, 128), F32)] + [like(v) for v in held],
        input_output_aliases={m + i: 2 + i for i in range(n)},
        scratch_shapes=([pltpu.VMEM((TOK, ROWS), BF16)] if halves else []) + [pltpu.VMEM((ROWS, 128), F32)],
        compiler_params=params(12),
        cost_estimate=COST,
        name="more_rows",
    )(*acts, anchor, *held)
    return k, rp, held


def add_rows(acc, k_ref, r):
    for b in range(RB):
        rb = spread(r[b:b + 1, :])
        for g in range(16):
            scale = jnp.concatenate([rb[8 * g:8 * g + 8, :]] * (COLS // 128), axis=1)
            acc = acc + k_ref[pl.ds(b * 128 + g * 8, 8), :] * scale
    return acc


PASS = pl.CostEstimate(flops=8 * ROWS * COLS, bytes_accessed=25_700_000, transcendentals=0)


def col_kernel(n, k0, k1, k2, k3, p0, p1, p2, p3, *refs):
    r_ref, cp_ref = refs[n:n + 2]
    r = (1.0 / FF) / (p0[...] + p1[...] + p2[...] + p3[...])
    r_ref[...] = r
    acc = jnp.zeros((8, COLS), F32)
    for s, k_ref in enumerate((k0, k1, k2, k3)):
        acc = add_rows(acc, k_ref, r[8 * s:8 * s + 8, :])
    cp_ref[...] = jnp.sum(acc, axis=0, keepdims=True)


def col_pass(ks, parts, *held):
    n = len(held)
    r, cp, *held = pl.pallas_call(
        functools.partial(col_kernel, n),
        in_specs=[VM] * 8 + [ANY] * n,
        out_specs=[VM] * 2 + [ANY] * n,
        out_shape=[jax.ShapeDtypeStruct((32, 128), F32), jax.ShapeDtypeStruct((1, COLS), F32)] + [like(v) for v in held],
        input_output_aliases={8 + i: 2 + i for i in range(n)},
        compiler_params=params(12),
        cost_estimate=PASS,
        name="column_sums",
    )(*ks, *parts, *held)
    return r, cp, held


def row_kernel(k0, k1, k2, k3, p0, p1, rp_ref, acc_ref, c_ref):
    c_ref[...] = jnp.broadcast_to((1.0 / FF) / (p0[...] + p1[...]), (8, COLS))
    rp_ref[...] = jnp.ones((32, 128), F32)
    for s, k_ref in enumerate((k0, k1, k2, k3)):
        for g in range(ROWS // 64):
            acc = [jnp.zeros((8, 128), F32) for _ in range(8)]
            for t in range(COLS // 128):
                c = c_ref[:, t * 128:(t + 1) * 128]
                for j in range(8):
                    acc[j] = acc[j] + k_ref[pl.ds(64 * g + 8 * j, 8), t * 128:(t + 1) * 128] * c
            for j in range(8):
                acc_ref[pl.ds(64 * g + 8 * j, 8), :] = acc[j]
        for b in range(RB):
            rp_ref[pl.ds(s * 8 + b, 1), :] = block_sums(acc_ref[pl.ds(b * 128, 128), :])


def row_pass(ks, cp, sib):
    return pl.pallas_call(
        row_kernel,
        in_specs=[VM] * 6,
        out_specs=VM,
        out_shape=jax.ShapeDtypeStruct((32, 128), F32),
        scratch_shapes=[pltpu.VMEM((ROWS, 128), F32), pltpu.VMEM((8, COLS), F32)],
        compiler_params=params(12),
        cost_estimate=PASS,
        name="row_sums",
    )(*ks, cp, sib)


def lay_kernel(place_ref, w0, w1, wlo, whi, w3, lhs_ref):
    core = place_ref[0]
    x = place_ref[1]
    for t, w in enumerate((w0, w1, None, w3)):
        at = lax.rem(x + 4 - t, 4) * 64
        for s in range(4):
            src, i = ((wlo, whi)[s // 2], s % 2) if t == 2 else (w, s)
            for e in range(2):
                for h in range(2):
                    half = 1 - core if h == 0 else core
                    lhs_ref[pl.ds(pl.multiple_of(h * 256 + at + e * 32, 32), 32), s * ROWS:(s + 1) * ROWS] = (
                        src[i, pl.ds(pl.multiple_of(32 * half, 32), 32), e * ROWS:(e + 1) * ROWS])


def lay(place, w):
    return pl.pallas_call(
        lay_kernel,
        in_specs=[SMEM] + [VM] * 5,
        out_specs=VM,
        out_shape=jax.ShapeDtypeStruct((512, 4 * ROWS), BF16),
        compiler_params=params(12),
        cost_estimate=pl.CostEstimate(flops=0, bytes_accessed=7_300_000, transcendentals=0),
        name="lay_weights",
    )(place, *w)


def join_kernel(lhs_ref, k0, k1, k2, k3, r_ref, c0_ref, c1_ref, sib_ref, own_ref, rb_ref):
    ks = (k0, k1, k2, k3)

    @pl.when(pl.program_id(0) == 0)
    def _():
        for s in range(4):
            for b in range(RB):
                rb_ref[pl.ds(s * ROWS + b * 128, 128), :] = spread(r_ref[pl.ds(s * 8 + b, 1), :] * FF)

    at = pl.multiple_of(pl.program_id(0) * CT, CT)
    c = (1.0 / FF) / (c0_ref[:, pl.ds(at, CT)] + c1_ref[:, pl.ds(at, CT)])
    total = None
    for s in range(4):
        rb = rb_ref[pl.ds(s * ROWS, ROWS), :]
        k = ks[s][:, pl.ds(at, CT)]
        p = jnp.concatenate(
            [(rb * k[:, h * 128:(h + 1) * 128] * c[:, h * 128:(h + 1) * 128]).astype(BF16) for h in range(CT // 128)], axis=1)
        d = jnp.dot(lhs_ref[:, s * ROWS:(s + 1) * ROWS], p, preferred_element_type=F32)
        total = d if total is None else total + d
    sib_ref[:, pl.ds(at, CT)] = total[:256].astype(BF16)
    own_ref[:, pl.ds(at, CT)] = total[256:].astype(BF16)


def join(lhs, ks, r, cp, sib):
    return pl.pallas_call(
        join_kernel,
        grid=(COLS // CT,),
        in_specs=[VM] * 8,
        out_specs=[VM, VM],
        out_shape=[jax.ShapeDtypeStruct((256, COLS), BF16)] * 2,
        scratch_shapes=[pltpu.VMEM((4 * ROWS, 128), F32)],
        compiler_params=params(12),
        cost_estimate=pl.CostEstimate(flops=2 * 512 * 4 * ROWS * COLS, bytes_accessed=20_000_000, transcendentals=0),
        name="join",
    )(lhs, *ks, r, cp, sib)


def add_kernel(own_ref, other_ref, out_ref):
    out_ref[0] = (own_ref[...].astype(F32) + other_ref[...].astype(F32)).astype(BF16)


def add(own, other):
    tile = pl.BlockSpec((32, COLS), lambda i: (i, 0))
    return pl.pallas_call(
        add_kernel,
        grid=(CLIENTS,),
        in_specs=[tile] * 2,
        out_specs=pl.BlockSpec((1, 32, COLS), lambda i: (i, 0, 0)),
        out_shape=jax.ShapeDtypeStruct((CLIENTS, 32, COLS), BF16),
        compiler_params=params(12),
        cost_estimate=pl.CostEstimate(flops=256 * COLS, bytes_accessed=2_800_000, transcendentals=0),
        name="add_cores",
    )(own, other)


def pick(x, index, axis):
    return lax.dynamic_index_in_dim(x, index, axis, keepdims=False)


def sum_over_clients(part, z):
    def at(s):
        return pick(part, lax.rem(z + 8 + s, 8), 0)

    def wide(v):
        return v.astype(F32)

    far = at(4)
    f1 = shift(far[:16], "client", -2)
    f2 = shift(far[16:], "client", 2)
    u3, u1 = shift(jnp.stack([at(-3), at(-1)]), "client", -1)
    d3, d1 = shift(jnp.stack([at(3), at(1)]), "client", 1)
    u = wide(at(-2)) + wide(u3)
    u = jnp.concatenate([u[:16] + wide(f1), u[16:]], 0).astype(BF16)
    d = wide(at(2)) + wide(d3)
    d = jnp.concatenate([d[:16], d[16:] + wide(f2)], 0).astype(BF16)
    u2 = shift(u, "client", -2)
    d2 = shift(d, "client", 2)
    return wide(at(0)) + wide(u1) + wide(d1) + wide(u2) + wide(d2)


def local(client_acts, anchor_acts, client_weights):
    z = lax.axis_index("client")
    y = lax.axis_index("y")
    core = lax.axis_index("core")
    x = lax.axis_index("col")

    w = client_weights[0].reshape(2, 4, 64, ROWS)
    half = lax.rem(z, 2)
    b_half = lax.dynamic_slice_in_dim(anchor_acts, 32 * half, 32, 0)

    def part(s):
        v = pick(w, lax.rem(y + s, 4), 1)
        return jnp.concatenate([v[0], v[1]], axis=1)

    m = [shift(jnp.concatenate([part(s), b_half], axis=0), "y", s) for s in (1, 2, 3)]
    a = [client_acts[0]] + [shift(client_acts[0], "col", s) for s in (1, 2, 3)]
    acts = jnp.concatenate(a, axis=0)

    b_mine = jnp.stack([v[64:] for v in m])
    pair = lax.ppermute(b_mine, "client", [(i, i ^ 1) for i in range(CLIENTS)])
    sib = shift(jnp.concatenate([anchor_acts.reshape(2, 32, COLS), b_mine, pair], axis=0), "core", 1)

    acts1, acts3 = shift(acts, "y", 1), shift(acts, "y", -1)
    lo2, hi2 = shift(acts1[:256], "y", 1), shift(acts3[256:], "y", -1)

    w = jnp.stack([part(0)] + [v[:64] for v in m])
    place = jnp.stack([lax.rem(x - y + 4, 4), core, half]).astype(jnp.int32)
    w1, w3 = shift(w, "col", 1), shift(w, "col", -1)
    k0, p0, anchor, (w1, w3) = first(place, acts, anchor_acts, m, pair, sib, w1, w3)
    w2 = [shift(w1[:2], "col", 1), shift(w3[2:], "col", -1)]

    k1, p1, _ = more([acts1], anchor)
    k3, p3, _ = more([acts3], anchor)
    k2, p2, _ = more([lo2, hi2], anchor)
    ks = [k0, k1, k2, k3]
    rp = jnp.concatenate([p0, p1, p2, p3], axis=0)

    held = w2
    for step in range(ITERS):
        r, cp, held = col_pass(ks, [rp] + [shift(rp, "col", s) for s in (1, 2, 3)], *held)
        sib = shift(cp, "core", 1)
        if step == 0:
            place = jnp.stack([core, x]).astype(jnp.int32)
            lhs = lay(place, [w, w1, *held, w3])
            held = []
        if step == 1:
            held = [lhs]
        if step < ITERS - 1:
            rp = row_pass(ks, cp, sib)

    sib, own = join(held[0], ks, r, cp, sib)
    part = add(own, shift(sib, "core", 1))
    return (sum_over_clients(part, z) / CLIENTS).astype(BF16)


def solution(mesh):
    mesh = Mesh(mesh.devices.reshape(8, 4, 2, 4), ("client", "y", "core", "col"))
    row = ("y", "core")
    in_specs = (P("client", "col", row), P(row, "col"), P("client", "col", row))
    out_specs = P(("client", "y", "core"), "col")
    return jax.shard_map(local, mesh=mesh, in_specs=in_specs, out_specs=out_specs, check_vma=False)
```

```python
import functools

import jax
import jax.numpy as jnp
from jax import lax
from jax.experimental import pallas as pl
from jax.experimental.pallas import tpu as pltpu
from jax.sharding import Mesh, PartitionSpec as P

FF = 7168
TOK = 512
ITERS = 3
CLIENTS = 8
entropic = 0.05

F32 = jnp.float32
BF16 = jnp.bfloat16
SIZES = {"client": 8, "y": 4, "core": 2, "col": 4}
ROWS = 896
COLS = 1792
RB = ROWS // 128
CT = 256


def shift(x, axis, s):
    n = SIZES[axis]
    return lax.ppermute(x, axis, [(i, (i + s) % n) for i in range(n)])


def params(mb):
    return pltpu.CompilerParams(vmem_limit_bytes=mb * 1024 * 1024)


VM = pl.BlockSpec(memory_space=pltpu.VMEM)
ANY = pl.BlockSpec(memory_space=pl.ANY)
SMEM = pl.BlockSpec(memory_space=pltpu.SMEM)


def like(v):
    return jax.ShapeDtypeStruct(v.shape, v.dtype)


def block_sums(block):
    return jnp.sum(block.T, axis=0, keepdims=True)


def tiles(acts_ref, anchor_ref, k_ref):
    for t in range(COLS // CT):
        sim = lax.dot_general(
            acts_ref[...], anchor_ref[:, t * CT:(t + 1) * CT],
            (((0,), (0,)), ((), ())), preferred_element_type=F32)
        k = jnp.exp(sim * (1.0 / (TOK * entropic)))
        k_ref[:, t * CT:(t + 1) * CT] = k
        yield t, k


def first_kernel(n, place_ref, acts_ref, b_ref, m1, m2, m3, pair_ref, sib_ref, *refs):
    k_ref, rp_ref, anchor_ref = refs[n:n + 3]
    acc_ref = refs[-1]
    off = place_ref[0]
    core = place_ref[1]
    half = place_ref[2]

    def put(s, of_core, of_half, value):
        at = lax.rem(s + off, 4) * 128 + 64 * of_core + 32 * of_half
        anchor_ref[pl.ds(pl.multiple_of(at, 32), value.shape[0]), :] = value

    put(0, core, 0, b_ref[...])
    put(0, 1 - core, 0, sib_ref[0])
    put(0, 1 - core, 1, sib_ref[1])
    for s, m in ((1, m1), (2, m2), (3, m3)):
        put(s, core, half, m[pl.ds(64, 32), :])
        put(s, core, 1 - half, pair_ref[s - 1])
        put(s, 1 - core, half, sib_ref[s + 1])
        put(s, 1 - core, 1 - half, sib_ref[s + 4])
    row_partials(acts_ref, anchor_ref, k_ref, rp_ref, acc_ref)


def row_partials(acts_ref, anchor_ref, k_ref, rp_ref, acc_ref):
    for t, k in tiles(acts_ref, anchor_ref, k_ref):
        part = k[:, :128] + k[:, 128:]
        if t == 0:
            acc_ref[...] = part
        else:
            acc_ref[...] += part
    for b in range(RB):
        rp_ref[pl.ds(b, 1), :] = block_sums(acc_ref[pl.ds(b * 128, 128), :])
    rp_ref[pl.ds(RB, 1), :] = jnp.ones((1, 128), F32)


K_SHAPE = jax.ShapeDtypeStruct((ROWS, COLS), F32)
COST = pl.CostEstimate(flops=2 * TOK * ROWS * COLS, bytes_accessed=10_000_000, transcendentals=ROWS * COLS)


def first(place, acts, b, m, pair, sib, *held):
    n = len(held)
    k, rp, anchor, *held = pl.pallas_call(
        functools.partial(first_kernel, n),
        in_specs=[SMEM] + [VM] * 7 + [ANY] * n,
        out_specs=[VM] * 3 + [ANY] * n,
        out_shape=[K_SHAPE, jax.ShapeDtypeStruct((8, 128), F32), jax.ShapeDtypeStruct((TOK, COLS), BF16)] + [like(v) for v in held],
        input_output_aliases={8 + i: 3 + i for i in range(n)},
        scratch_shapes=[pltpu.VMEM((ROWS, 128), F32)],
        compiler_params=params(12),
        cost_estimate=COST,
        name="similarity",
    )(place, acts, b, *m, pair, sib, *held)
    return k, rp, anchor, held


def spread(r):
    return jnp.broadcast_to(r, (128, 128)).T


def more_kernel(n, acts_ref, anchor_ref, *refs):
    k_ref, rp_ref = refs[n:n + 2]
    row_partials(acts_ref, anchor_ref, k_ref, rp_ref, refs[-1])


def more_halves_kernel(n, lo_ref, hi_ref, anchor_ref, *refs):
    k_ref, rp_ref = refs[n:n + 2]
    acts_ref, acc_ref = refs[-2:]
    acts_ref[pl.ds(0, TOK // 2), :] = lo_ref[...]
    acts_ref[pl.ds(TOK // 2, TOK // 2), :] = hi_ref[...]
    row_partials(acts_ref, anchor_ref, k_ref, rp_ref, acc_ref)


def more(acts, anchor, *held):
    n = len(held)
    halves = len(acts) == 2
    m = len(acts) + 1
    k, rp, *held = pl.pallas_call(
        functools.partial(more_halves_kernel if halves else more_kernel, n),
        in_specs=[VM] * m + [ANY] * n,
        out_specs=[VM] * 2 + [ANY] * n,
        out_shape=[K_SHAPE, jax.ShapeDtypeStruct((8, 128), F32)] + [like(v) for v in held],
        input_output_aliases={m + i: 2 + i for i in range(n)},
        scratch_shapes=([pltpu.VMEM((TOK, ROWS), BF16)] if halves else []) + [pltpu.VMEM((ROWS, 128), F32)],
        compiler_params=params(12),
        cost_estimate=COST,
        name="more_rows",
    )(*acts, anchor, *held)
    return k, rp, held


def add_rows(acc, k_ref, r):
    for b in range(RB):
        rb = spread(r[b:b + 1, :])
        for g in range(16):
            scale = jnp.concatenate([rb[8 * g:8 * g + 8, :]] * (COLS // 128), axis=1)
            acc = acc + k_ref[pl.ds(b * 128 + g * 8, 8), :] * scale
    return acc


PASS = pl.CostEstimate(flops=8 * ROWS * COLS, bytes_accessed=25_700_000, transcendentals=0)


def col_kernel(n, k0, k1, k2, k3, p0, p1, p2, p3, *refs):
    r_ref, cp_ref = refs[n:n + 2]
    r = (1.0 / FF) / (p0[...] + p1[...] + p2[...] + p3[...])
    r_ref[...] = r
    acc = jnp.zeros((8, COLS), F32)
    for s, k_ref in enumerate((k0, k1, k2, k3)):
        acc = add_rows(acc, k_ref, r[8 * s:8 * s + 8, :])
    cp_ref[...] = jnp.sum(acc, axis=0, keepdims=True)


def col_pass(ks, parts, *held):
    n = len(held)
    r, cp, *held = pl.pallas_call(
        functools.partial(col_kernel, n),
        in_specs=[VM] * 8 + [ANY] * n,
        out_specs=[VM] * 2 + [ANY] * n,
        out_shape=[jax.ShapeDtypeStruct((32, 128), F32), jax.ShapeDtypeStruct((1, COLS), F32)] + [like(v) for v in held],
        input_output_aliases={8 + i: 2 + i for i in range(n)},
        compiler_params=params(12),
        cost_estimate=PASS,
        name="column_sums",
    )(*ks, *parts, *held)
    return r, cp, held


def row_kernel(k0, k1, k2, k3, p0, p1, rp_ref, acc_ref, c_ref):
    c_ref[...] = jnp.broadcast_to((1.0 / FF) / (p0[...] + p1[...]), (8, COLS))
    rp_ref[...] = jnp.ones((32, 128), F32)
    for s, k_ref in enumerate((k0, k1, k2, k3)):
        for g in range(ROWS // 64):
            acc = [jnp.zeros((8, 128), F32) for _ in range(8)]
            for t in range(COLS // 128):
                c = c_ref[:, t * 128:(t + 1) * 128]
                for j in range(8):
                    acc[j] = acc[j] + k_ref[pl.ds(64 * g + 8 * j, 8), t * 128:(t + 1) * 128] * c
            for j in range(8):
                acc_ref[pl.ds(64 * g + 8 * j, 8), :] = acc[j]
        for b in range(RB):
            rp_ref[pl.ds(s * 8 + b, 1), :] = block_sums(acc_ref[pl.ds(b * 128, 128), :])


def row_pass(ks, cp, sib):
    return pl.pallas_call(
        row_kernel,
        in_specs=[VM] * 6,
        out_specs=VM,
        out_shape=jax.ShapeDtypeStruct((32, 128), F32),
        scratch_shapes=[pltpu.VMEM((ROWS, 128), F32), pltpu.VMEM((8, COLS), F32)],
        compiler_params=params(12),
        cost_estimate=PASS,
        name="row_sums",
    )(*ks, cp, sib)


def lay_kernel(place_ref, w0, w1, wlo, whi, w3, lhs_ref):
    core = place_ref[0]
    x = place_ref[1]
    for t, w in enumerate((w0, w1, None, w3)):
        at = lax.rem(x + 4 - t, 4) * 64
        for s in range(4):
            src, i = ((wlo, whi)[s // 2], s % 2) if t == 2 else (w, s)
            for e in range(2):
                for h in range(2):
                    half = 1 - core if h == 0 else core
                    lhs_ref[pl.ds(pl.multiple_of(h * 256 + at + e * 32, 32), 32), s * ROWS:(s + 1) * ROWS] = (
                        src[i, pl.ds(pl.multiple_of(32 * half, 32), 32), e * ROWS:(e + 1) * ROWS])


def lay(place, w):
    return pl.pallas_call(
        lay_kernel,
        in_specs=[SMEM] + [VM] * 5,
        out_specs=VM,
        out_shape=jax.ShapeDtypeStruct((512, 4 * ROWS), BF16),
        compiler_params=params(12),
        cost_estimate=pl.CostEstimate(flops=0, bytes_accessed=7_300_000, transcendentals=0),
        name="lay_weights",
    )(place, *w)


def join_kernel(lhs_ref, k0, k1, k2, k3, r_ref, c0_ref, c1_ref, sib_ref, own_ref, rb_ref):
    ks = (k0, k1, k2, k3)

    @pl.when(pl.program_id(0) == 0)
    def _():
        for s in range(4):
            for b in range(RB):
                rb_ref[pl.ds(s * ROWS + b * 128, 128), :] = spread(r_ref[pl.ds(s * 8 + b, 1), :] * FF)

    at = pl.multiple_of(pl.program_id(0) * CT, CT)
    c = (1.0 / FF) / (c0_ref[:, pl.ds(at, CT)] + c1_ref[:, pl.ds(at, CT)])
    total = None
    for s in range(4):
        rb = rb_ref[pl.ds(s * ROWS, ROWS), :]
        k = ks[s][:, pl.ds(at, CT)]
        p = jnp.concatenate(
            [(rb * k[:, h * 128:(h + 1) * 128] * c[:, h * 128:(h + 1) * 128]).astype(BF16) for h in range(CT // 128)], axis=1)
        d = jnp.dot(lhs_ref[:, s * ROWS:(s + 1) * ROWS], p, preferred_element_type=F32)
        total = d if total is None else total + d
    sib_ref[:, pl.ds(at, CT)] = total[:256].astype(BF16)
    own_ref[:, pl.ds(at, CT)] = total[256:].astype(BF16)


def join(lhs, ks, r, cp, sib):
    return pl.pallas_call(
        join_kernel,
        grid=(COLS // CT,),
        in_specs=[VM] * 8,
        out_specs=[VM, VM],
        out_shape=[jax.ShapeDtypeStruct((256, COLS), BF16)] * 2,
        scratch_shapes=[pltpu.VMEM((4 * ROWS, 128), F32)],
        compiler_params=params(12),
        cost_estimate=pl.CostEstimate(flops=2 * 512 * 4 * ROWS * COLS, bytes_accessed=20_000_000, transcendentals=0),
        name="join",
    )(lhs, *ks, r, cp, sib)


def add_kernel(own_ref, other_ref, out_ref):
    out_ref[0] = (own_ref[...].astype(F32) + other_ref[...].astype(F32)).astype(BF16)


def add(own, other):
    tile = pl.BlockSpec((32, COLS), lambda i: (i, 0))
    return pl.pallas_call(
        add_kernel,
        grid=(CLIENTS,),
        in_specs=[tile] * 2,
        out_specs=pl.BlockSpec((1, 32, COLS), lambda i: (i, 0, 0)),
        out_shape=jax.ShapeDtypeStruct((CLIENTS, 32, COLS), BF16),
        compiler_params=params(12),
        cost_estimate=pl.CostEstimate(flops=256 * COLS, bytes_accessed=2_800_000, transcendentals=0),
        name="add_cores",
    )(own, other)


def pick(x, index, axis):
    return lax.dynamic_index_in_dim(x, index, axis, keepdims=False)


def sum_over_clients(part, z):
    def at(s):
        return pick(part, lax.rem(z + 8 + s, 8), 0)

    def wide(v):
        return v.astype(F32)

    far = at(4)
    f1 = shift(far[:16], "client", -2)
    f2 = shift(far[16:], "client", 2)
    u3 = shift(at(-3), "client", -1)
    d3 = shift(at(3), "client", 1)
    u = wide(at(-2)) + wide(u3)
    u = jnp.concatenate([u[:16] + wide(f1), u[16:]], 0).astype(BF16)
    d = wide(at(2)) + wide(d3)
    d = jnp.concatenate([d[:16], d[16:] + wide(f2)], 0).astype(BF16)
    u2 = shift(u, "client", -2)
    d2 = shift(d, "client", 2)
    u1 = shift(at(-1), "client", -1)
    d1 = shift(at(1), "client", 1)
    return wide(at(0)) + wide(u1) + wide(d1) + wide(u2) + wide(d2)


def local(client_acts, anchor_acts, client_weights):
    z = lax.axis_index("client")
    y = lax.axis_index("y")
    core = lax.axis_index("core")
    x = lax.axis_index("col")

    w = client_weights[0].reshape(2, 4, 64, ROWS)
    half = lax.rem(z, 2)
    b_half = lax.dynamic_slice_in_dim(anchor_acts, 32 * half, 32, 0)

    def part(s):
        v = pick(w, lax.rem(y + s, 4), 1)
        return jnp.concatenate([v[0], v[1]], axis=1)

    m = [shift(jnp.concatenate([part(s), b_half], axis=0), "y", s) for s in (1, 2, 3)]
    a = [client_acts[0]] + [shift(client_acts[0], "col", s) for s in (1, 2, 3)]
    acts = jnp.concatenate(a, axis=0)

    b_mine = jnp.stack([v[64:] for v in m])
    pair = lax.ppermute(b_mine, "client", [(i, i ^ 1) for i in range(CLIENTS)])
    sib = shift(jnp.concatenate([anchor_acts.reshape(2, 32, COLS), b_mine, pair], axis=0), "core", 1)

    acts1, acts3 = shift(acts, "y", 1), shift(acts, "y", -1)
    lo2, hi2 = shift(acts1[:256], "y", 1), shift(acts3[256:], "y", -1)

    w = jnp.stack([part(0)] + [v[:64] for v in m])
    place = jnp.stack([lax.rem(x - y + 4, 4), core, half]).astype(jnp.int32)
    w1, w3 = shift(w, "col", 1), shift(w, "col", -1)
    k0, p0, anchor, (w1, w3) = first(place, acts, anchor_acts, m, pair, sib, w1, w3)
    w2 = [shift(w1[:2], "col", 1), shift(w3[2:], "col", -1)]

    k1, p1, _ = more([acts1], anchor)
    k3, p3, _ = more([acts3], anchor)
    k2, p2, _ = more([lo2, hi2], anchor)
    ks = [k0, k1, k2, k3]
    rp = jnp.concatenate([p0, p1, p2, p3], axis=0)

    held = w2
    for step in range(ITERS):
        r, cp, held = col_pass(ks, [rp] + [shift(rp, "col", s) for s in (1, 2, 3)], *held)
        sib = shift(cp, "core", 1)
        if step == 0:
            place = jnp.stack([core, x]).astype(jnp.int32)
            lhs = lay(place, [w, w1, *held, w3])
            held = []
        if step == 1:
            held = [lhs]
        if step < ITERS - 1:
            rp = row_pass(ks, cp, sib)

    sib, own = join(held[0], ks, r, cp, sib)
    part = add(own, shift(sib, "core", 1))
    return (sum_over_clients(part, z) / CLIENTS).astype(BF16)


def solution(mesh):
    mesh = Mesh(mesh.devices.reshape(8, 4, 2, 4), ("client", "y", "core", "col"))
    row = ("y", "core")
    in_specs = (P("client", "col", row), P(row, "col"), P("client", "col", row))
    out_specs = P(("client", "y", "core"), "col")
    return jax.shard_map(local, mesh=mesh, in_specs=in_specs, out_specs=out_specs, check_vma=False)
```
